128 devices in a mesh: expert: 32 (over x, y, core), tensor: 4 (over z).
Axes of the slice: x: 4, y: 4, z: 4, core: 2. Of those that a mesh axis runs over, the one named last changes fastest.
Arguments:
- hidden_in: bfloat16 [768, 7168], P('expert', 'tensor'), may hold values from -6 to 6
- norm_gain: float32 [2, 7168], P(None, 'tensor'), may hold values from 0.25 to 1.75
- router: float32 [2, 7168, 32], P(None, 'tensor'), may hold values from -0.0625 to 0.0625
- w_gate: bfloat16 [2, 32, 7168, 1024], P(None, 'expert', None, 'tensor'), may hold values from -0.0625 to 0.0625
- w_up: bfloat16 [2, 32, 7168, 1024], P(None, 'expert', None, 'tensor'), may hold values from -0.0625 to 0.0625
- w_down: bfloat16 [2, 32, 1024, 7168], P(None, 'expert', 'tensor'), may hold values from -0.1875 to 0.1875
- routes: int32 [2, 768, 8], P(None, 'expert'), may hold values from 0 to 31, all different within a row; in each aligned block of 24 rows (0 to 23, 24 to 47, ..., all dimensions but the last counted through in order) at most 12 rows name the same one
Outputs:
- hidden_out: bfloat16 [768, 7168], P('expert', 'tensor')
The draws below stay inside these ranges and needn't reach their ends.
Inputs may be any that keep to these rules, and one draw needn't show every extreme that they name: `routes`: each token names 8 different experts in each layer. Among the 24 tokens of one index of expert (aligned blocks of rows of one layer), no expert is named by more than 12 tokens, a bound that some block reaches.
All inputs are finite; a program needn't handle non-finite values.
Results may differ from the reference program's by a relative error of at most 0.018.
Values may be sent and summed in bfloat16 or wider, within the bound.
No kernel may reach another device: no remote copies, remote signals or barrier semaphores. Data moves between devices by JAX's collectives and lax.ppermute only.
A program may use at most 128 MiB of HBM per device.

```python
import math
import jax
import jax.numpy as jnp
import numpy as np
from jax import lax

D = 7168
FF = 1024
TOP = 8
LAYERS = 2
TOK_DEV = 24
EXPERTS = 32
CAP = 12
TOKENS = 768
N_EXPERT = 32
N_TENSOR = 4


def block_levels(rng, extent, pieces, smallest, high):
    level, own = 1.0, jax.random.fold_in(rng, 6)
    for position, blocks in pieces:
        steps = jnp.exp(jax.random.uniform(jax.random.fold_in(own, position), (blocks,), jnp.float32, smallest / len(pieces), high / len(pieces)))
        level = level * jnp.repeat(steps, extent[position] // blocks).reshape([-1 if axis == position else 1 for axis in range(len(extent))])
    return level


def assign_block(stream_key, own, number, rows, count, top, most, slope):
    ranking = jax.random.permutation(stream_key, count)
    heavy_load, common = portions_of(count, rows * top, most, slope, True), portions_of(count, rows * top, most, slope, False)
    places = jnp.arange(count)

    def named(sizes, rotation):
        used = int((sizes > 0).sum())
        fixed = max(1, used // 4)
        shifted = fixed + (places - fixed + rotation * (used - fixed)) % max(1, count - fixed)
        return jnp.zeros((count,), jnp.int32).at[ranking[jnp.where(places < fixed, places, shifted)]].set(jnp.asarray(sizes, jnp.int32))

    sizes = jnp.where(number % 4 == 0, named(heavy_load, number // 4), named(common, number - number // 4 - 1))
    mixed = jax.random.permutation(jax.random.fold_in(own, 3), count)
    giver, taker = mixed[0:count // 2 * 2:2], mixed[1:count // 2 * 2:2]
    room = jnp.minimum(sizes[giver] - 1, most - sizes[taker]) // 2
    room = jnp.where((giver == ranking[0]) | (taker == ranking[0]) | (sizes[taker] == 0), 0, jnp.maximum(room, 0))
    shifted = jax.random.randint(jax.random.fold_in(own, 4), (count // 2,), 0, 1 << 20) % (room + 1)
    sizes = sizes.at[giver].add(-shifted).at[taker].add(shifted)
    items = jnp.searchsorted(jnp.cumsum(sizes), jnp.arange(rows * top), side="right").astype(jnp.int32)
    table = items.reshape(top, rows).T
    table = table[jax.random.permutation(jax.random.fold_in(own, 1), rows)]
    rotation = jax.random.randint(jax.random.fold_in(own, 2), (rows, 1), 0, top)
    return jnp.take_along_axis(table, (jnp.arange(top)[None, :] + rotation) % top, axis=1)


def portions_of(count, total, most, skew, full):
    loads = [(1 << 20) // math.isqrt(grade ** skew) + 1 for grade in range(1, count + 1)]
    largest = most if full else min(most, max(-(-total // count), total * loads[0] // sum(loads)))
    least = 1 if total - largest >= count - 1 else 0
    holding, surplus = [largest] + [least] * (count - 1), total - largest - least * (count - 1)
    while surplus > 0:
        free = [i for i in range(1, count) if holding[i] < largest] or [i for i in range(1, count) if holding[i] < most]
        pool, remaining = sum([loads[i] for i in free]), surplus
        for i in free:
            extra = min(most - holding[i], max(1, remaining * loads[i] // pool), surplus)
            holding[i] = holding[i] + extra
            surplus = surplus - extra
    return np.array(holding)


def bell_draw(stream_key, shape, width, limit, pieces=(), held_as=jnp.bfloat16):
    array = width * jax.random.normal(stream_key, shape, jnp.float32)
    if pieces:
        array = array * block_levels(stream_key, shape, pieces, -0.22, 0.18)
    return jnp.clip(array, -limit, limit).astype(held_as)


def setup_inputs(seed: int = 0) -> dict:
    arg_keys = jax.random.split(jax.random.key(seed), 8)
    hidden_in = bell_draw(arg_keys[0], (TOKENS, D), 1.0, 6.0, ((0, 32), (1, 4)))
    norm_gain = jnp.clip(1.0 + 0.15 * jax.random.normal(arg_keys[1], (LAYERS, D), jnp.float32), 0.25, 1.75)
    router = bell_draw(arg_keys[2], (LAYERS, D, EXPERTS), D ** -0.5, 0.0625, ((1, 4),), jnp.float32)
    w_gate = bell_draw(arg_keys[3], (LAYERS, EXPERTS, D, FF), D ** -0.5, 0.0625, ((1, 32), (3, 4)))
    w_up = bell_draw(arg_keys[4], (LAYERS, EXPERTS, D, FF), D ** -0.5, 0.0625, ((1, 32), (3, 4)))
    w_down = bell_draw(arg_keys[5], (LAYERS, EXPERTS, FF, D), FF ** -0.5, 0.1875, ((1, 32), (2, 4)))
    routes_keys = jax.random.split(jax.random.fold_in(arg_keys[6], 1), LAYERS * TOKENS // TOK_DEV)
    routes_turns = jax.random.permutation(jax.random.fold_in(arg_keys[6], 3), LAYERS * TOKENS // TOK_DEV)
    routes = jax.vmap(lambda own, number: assign_block(jax.random.fold_in(arg_keys[6], 2), own, number, TOK_DEV, EXPERTS, TOP, CAP, 2))(routes_keys, routes_turns).reshape((LAYERS, TOKENS, TOP))
    return {"hidden_in": hidden_in, "norm_gain": norm_gain, "router": router, "w_gate": w_gate, "w_up": w_up, "w_down": w_down, "routes": routes}


route_scale = 2.5

def moe_layer(state, gain, router, w_gate, w_up, w_down, chosen):
    values = state.astype(jnp.float32)
    mean_square = lax.optimization_barrier(jnp.mean(values * values, axis=1))
    normed = (values * lax.rsqrt(mean_square + 1e-06)[:, None] * gain[None, :]).astype(jnp.bfloat16)
    scores = jnp.dot(normed.astype(jnp.float32), router, precision=lax.Precision.HIGHEST)
    probs = jax.nn.sigmoid(scores)
    picked_probs = jnp.take_along_axis(probs, chosen, axis=1)
    weights = route_scale * picked_probs / lax.optimization_barrier(jnp.sum(picked_probs, axis=1, keepdims=True))
    slots_each = N_EXPERT * CAP
    flat = chosen.reshape(N_EXPERT, TOK_DEV * TOP)
    picks = (flat[:, :, None] == jnp.arange(EXPERTS, dtype=jnp.int32)[None, None, :]).astype(jnp.int32)
    ranks = (jnp.cumsum(picks, axis=1) - picks).astype(jnp.int32)
    rank_each = lax.optimization_barrier(jnp.sum(ranks * picks, axis=2)).astype(jnp.int32)
    source = jnp.arange(N_EXPERT, dtype=jnp.int32)[:, None]
    slot = (flat * slots_each + source * CAP + rank_each).astype(jnp.int32)
    owner = jnp.repeat(jnp.arange(TOKENS, dtype=jnp.int32), TOP).reshape(N_EXPERT, TOK_DEV * TOP)
    table = jnp.full((EXPERTS * slots_each,), TOKENS, jnp.int32).at[slot.reshape(-1)].set(owner.reshape(-1))
    padded = jnp.concatenate([normed, jnp.zeros((1, D), jnp.bfloat16)], axis=0)
    part = FF // N_TENSOR

    def one_expert(index):
        rows = padded[lax.dynamic_slice_in_dim(table, index * slots_each, slots_each)]
        gate = jnp.dot(rows, w_gate[index], preferred_element_type=jnp.float32)
        up = jnp.dot(rows, w_up[index], preferred_element_type=jnp.float32)
        act = (jax.nn.silu(gate) * up).astype(jnp.bfloat16)
        down = w_down[index]
        total = jnp.zeros((slots_each, D), jnp.float32)
        for quarter in range(N_TENSOR):
            partial_sum = jnp.dot(act[:, quarter * part:(quarter + 1) * part], down[quarter * part:(quarter + 1) * part], preferred_element_type=jnp.float32)
            total = total + lax.optimization_barrier(partial_sum.astype(jnp.bfloat16)).astype(jnp.float32)
        return total.astype(jnp.bfloat16)
    outputs = lax.map(one_expert, jnp.arange(EXPERTS, dtype=jnp.int32)).reshape(EXPERTS * slots_each, D)
    gathered = outputs[slot.reshape(-1)].reshape(TOKENS, TOP, D).astype(jnp.float32)
    mixed = lax.optimization_barrier(jnp.sum(weights[:, :, None] * gathered, axis=1))
    return (values + mixed).astype(jnp.bfloat16)

def reference(hidden_in, norm_gain, router, w_gate, w_up, w_down, routes):
    state = hidden_in
    for layer in range(LAYERS):
        state = moe_layer(state, norm_gain[layer], router[layer], w_gate[layer], w_up[layer], w_down[layer], routes[layer])
    return state
```

```python
import jax
import jax.numpy as jnp
from jax import lax
from jax.sharding import PartitionSpec as P

route_scale = 2.5
bf16, f32 = jnp.bfloat16, jnp.float32


def short(values):
    return lax.reduce_precision(values, 8, 7)


def thirds(values):
    high = short(values)
    middle = short(values - high)
    return [part.astype(bf16) for part in (high, middle, values - high - middle)]


def body(hidden_in, norm_gain, router, w_gate, w_up, w_down, routes):
    rows, part = hidden_in.shape
    layers, width, units = w_gate.shape[0], w_gate.shape[2], w_gate.shape[3]
    experts = router.shape[2]
    quarters = lax.axis_size("tensor")
    capacity = min(rows, 2 * rows * routes.shape[2] // experts)
    slots = experts * capacity
    me = lax.axis_index("expert")

    gains = jnp.stack(thirds(norm_gain), axis=0).reshape(3 * layers, part)
    opening = jnp.concatenate([hidden_in, gains, jnp.zeros((2, part), bf16)], axis=0)
    opening = lax.all_gather(opening, "tensor", axis=1, tiled=True)
    full = opening[:rows]
    gains = opening[rows : rows + 3 * layers].astype(f32).reshape(3, layers, width)
    gains = gains[0] + gains[1] + gains[2]

    state = hidden_in
    for layer in range(layers):
        down = w_down[layer, 0].reshape(units, quarters, part).transpose(1, 0, 2)
        down = lax.all_to_all(down, "tensor", split_axis=0, concat_axis=0)
        down = down.reshape(quarters * units, part)

        if layer:
            full = lax.all_gather(state, "tensor", axis=1, tiled=True)
        values = full.astype(f32)
        scale = lax.rsqrt(jnp.sum(values * values, axis=1) / width + 1e-06)
        normed = (values * scale[:, None] * gains[layer][None, :]).astype(bf16)

        chosen = routes[layer]
        expert_iota = lax.broadcasted_iota(jnp.int32, (1, 1, experts), 2)
        picks = jnp.any(chosen[:, :, None] == expert_iota, axis=1)
        earlier = lax.broadcasted_iota(jnp.int32, (rows, rows), 0) > lax.broadcasted_iota(
            jnp.int32, (rows, rows), 1
        )
        ranks = jnp.dot(earlier.astype(bf16), picks.astype(bf16), preferred_element_type=f32)
        marks = jnp.where(picks, ranks + 1.0, 0.0)
        marks_sent = jnp.pad(marks, ((0, 0), (0, 128 - experts))).astype(bf16)

        sent = jnp.concatenate([normed, marks_sent], axis=1)
        arrived = lax.all_gather(sent, "expert", axis=0, tiled=True)

        own = state.astype(f32) * scale[:, None] * norm_gain[layer][None, :]
        own = own.astype(bf16).astype(f32)
        scores = jnp.dot(own, router[layer], precision=lax.Precision.HIGHEST)
        probs = jax.nn.sigmoid(lax.psum(scores, "tensor"))
        picked = jnp.where(picks, probs, 0.0)
        weights = route_scale * picked / jnp.sum(picked, axis=1, keepdims=True)
        slot_iota = lax.broadcasted_iota(jnp.int32, (1, 1, capacity), 2).astype(f32) + 1.0
        mixer = jnp.where(marks[:, :, None] == slot_iota, weights[:, :, None], 0.0)
        mixer = mixer.reshape(rows, slots)
        mixer = jnp.concatenate(thirds(mixer)[:2], axis=0)

        tokens = arrived[:, :width]
        gate = jnp.dot(tokens, w_gate[layer, 0], preferred_element_type=f32)
        up = jnp.dot(tokens, w_up[layer, 0], preferred_element_type=f32)
        act = (jax.nn.silu(gate) * up).astype(bf16)
        mine = lax.broadcasted_iota(jnp.int32, (1, 128), 1) == me
        mark = jnp.sum(jnp.where(mine, arrived[:, width:].astype(f32), 0.0), axis=1)
        total = mark.shape[0]
        slot = lax.broadcasted_iota(jnp.int32, (slots, total), 0)
        token = lax.broadcasted_iota(jnp.int32, (slots, total), 1)
        inside = (slot // capacity) == (token // rows)
        taken = inside & ((slot % capacity + 1).astype(f32) == mark[None, :])
        act = jnp.dot(taken.astype(bf16), act, preferred_element_type=f32).astype(bf16)

        act = lax.all_gather(act, "tensor", axis=1, tiled=True)
        out = jnp.dot(act, down, preferred_element_type=f32).astype(bf16)
        returned = lax.all_to_all(
            out.reshape(experts, capacity, part), "expert", split_axis=0, concat_axis=0
        ).reshape(slots, part)
        mixed = jnp.dot(mixer, returned, preferred_element_type=f32)
        state = (state.astype(f32) + mixed[:rows] + mixed[rows:]).astype(bf16)
    return state


def solution(mesh):
    placed = (
        P("expert", "tensor"),
        P(None, "tensor"),
        P(None, "tensor", None),
        P(None, "expert", None, "tensor"),
        P(None, "expert", None, "tensor"),
        P(None, "expert", "tensor", None),
        P(None, "expert", None),
    )
    return jax.shard_map(
        body, mesh=mesh, in_specs=placed, out_specs=P("expert", "tensor"), check_vma=False
    )
```

```python
import jax
import jax.numpy as jnp
from jax import lax
from jax.experimental import pallas as pl
from jax.experimental.pallas import tpu as pltpu
from jax.sharding import PartitionSpec as P

route_scale = 2.5
bf16, f32 = jnp.bfloat16, jnp.float32

Y_STEPS = ((2, 6), (6, 2))
X_STEPS = ((8, 24), (24, 8))
SIBLING = (1, 1)


def short(values):
    return lax.reduce_precision(values, 8, 7)


def thirds(values):
    high = short(values)
    middle = short(values - high)
    return [part.astype(bf16) for part in (high, middle, values - high - middle)]


def swap(block, masks):
    count = lax.axis_size("expert")
    return lax.ppermute(block, "expert", [(i, i ^ masks[i & 1]) for i in range(count)])


def z_swap(block, step):
    pairs = []
    for i in range(lax.axis_size("expert")):
        mask = ((1, 3), (3, 1))[i & 1][step]
        pairs += [(i * 4 + z, i * 4 + (z ^ mask)) for z in range(4)]
    return lax.ppermute(block, ("expert", "tensor"), pairs)


def after(block, *others):
    return lax.optimization_barrier((block, *others))[0]


def gate_up_kernel(own_ref, other_ref, gate_ref, up_ref, out_ref):
    rows, units = own_ref.shape[0], gate_ref.shape[-1]

    @pl.when(pl.program_id(0) == 0)
    def _():
        out_ref[...] = jnp.zeros_like(out_ref)

    for start, tokens in ((0, own_ref), (rows, other_ref)):
        for first, weights in ((0, gate_ref), (units, up_ref)):
            out_ref[start : start + rows, first : first + units] += jnp.dot(
                tokens[...], weights[0, 0], preferred_element_type=f32
            )


def gate_up(own, other, w_gate, w_up, layer, first, width):
    depth = 512
    rows, units = own.shape[0], w_gate.shape[-1]
    tokens = pl.BlockSpec((rows, depth), lambda k: (0, k))
    weights = pl.BlockSpec((1, 1, depth, units), lambda k: (layer, 0, first // depth + k, 0))
    return pl.pallas_call(
        gate_up_kernel,
        grid=(width // depth,),
        in_specs=[tokens, tokens, weights, weights],
        out_specs=pl.BlockSpec((2 * rows, 2 * units), lambda k: (0, 0)),
        out_shape=jax.ShapeDtypeStruct((2 * rows, 2 * units), f32),
        cost_estimate=pl.CostEstimate(
            flops=8 * rows * width * units,
            bytes_accessed=4 * (rows + units) * width + 16 * rows * units,
            transcendentals=0,
        ),
    )(own, other, w_gate, w_up)


def down_kernel(z_ref, a0, a1, a2, w0, w1, w2, out_ref):
    total = jnp.dot(a0[...], w0[0, 0], preferred_element_type=f32)
    total += jnp.dot(a1[...], w1[0], preferred_element_type=f32)
    total += jnp.dot(a2[0], w2[0], preferred_element_type=f32)
    total += jnp.dot(a2[1], w2[1], preferred_element_type=f32)
    out_ref[...] = total.astype(out_ref.dtype)


def down_product(z, acts, w_down, layer, first, second):
    slots, units = acts[0].shape
    part = first.shape[-1]
    columns = 256
    steps = part // columns
    return pl.pallas_call(
        down_kernel,
        grid_spec=pltpu.PrefetchScalarGridSpec(
            num_scalar_prefetch=1,
            grid=(steps,),
            in_specs=[
                pl.BlockSpec((slots, units), lambda n, z: (0, 0)),
                pl.BlockSpec((slots, units), lambda n, z: (0, 0)),
                pl.BlockSpec((2, slots, units), lambda n, z: (0, 0, 0)),
                pl.BlockSpec((1, 1, units, columns), lambda n, z: (layer, 0, 0, z[0] * steps + n)),
                pl.BlockSpec((1, units, columns), lambda n, z: (0, 0, n)),
                pl.BlockSpec((2, units, columns), lambda n, z: (0, 0, n)),
            ],
            out_specs=pl.BlockSpec((slots, columns), lambda n, z: (0, n)),
        ),
        out_shape=jax.ShapeDtypeStruct((slots, part), bf16),
        cost_estimate=pl.CostEstimate(
            flops=8 * slots * units * part,
            bytes_accessed=8 * units * (slots + part) + 2 * slots * part,
            transcendentals=0,
        ),
    )(jnp.full((1,), z, jnp.int32), *acts, w_down, first, second)


def body(hidden_in, norm_gain, router, w_gate, w_up, w_down, routes):
    rows, part = hidden_in.shape
    layers, width, units = w_gate.shape[0], w_gate.shape[2], w_gate.shape[3]
    experts = router.shape[2]
    capacity = min(rows, 2 * rows * routes.shape[2] // experts)
    slots = experts * capacity
    chips = experts // 2
    half = width // 2
    me = lax.axis_index("expert")
    core = me & 1
    z = lax.axis_index("tensor")

    gains = jnp.stack(thirds(norm_gain), axis=0).reshape(3 * layers, part)
    opening = jnp.concatenate([hidden_in, gains, jnp.zeros((2, part), bf16)], axis=0)
    opening = lax.all_gather(opening, "tensor", axis=1, tiled=True)
    full = opening[:rows]
    gains = opening[rows : rows + 3 * layers].astype(f32).reshape(3, layers, width)
    gains = gains[0] + gains[1] + gains[2]

    bits = jnp.arange(chips, dtype=jnp.int32)
    sources = []
    for c in range(2):
        masks = [Y_STEPS[0][c], Y_STEPS[1][c], X_STEPS[0][c], X_STEPS[1][c]]
        total = jnp.zeros_like(bits)
        for n, mask in enumerate(masks):
            total = total ^ jnp.where(((bits >> n) & 1) == 1, mask, 0)
        sources.append(total)
    own_source = me ^ jnp.where(core == 1, sources[1], sources[0])
    other_source = (me ^ 1) ^ jnp.where(core == 1, sources[0], sources[1])
    source = jnp.repeat(jnp.concatenate([own_source, other_source]), rows)

    state = hidden_in
    for layer in range(layers):
        if layer:
            full = lax.all_gather(state, "tensor", axis=1, tiled=True)
        values = full.astype(f32)
        scale = lax.rsqrt(jnp.sum(values * values, axis=1) / width + 1e-06)
        normed = (values * scale[:, None] * gains[layer][None, :]).astype(bf16)

        chosen = routes[layer]
        expert_iota = lax.broadcasted_iota(jnp.int32, (1, 1, experts), 2)
        picks = jnp.any(chosen[:, :, None] == expert_iota, axis=1)
        earlier = lax.broadcasted_iota(jnp.int32, (rows, rows), 0) > lax.broadcasted_iota(
            jnp.int32, (rows, rows), 1
        )
        ranks = jnp.dot(earlier.astype(bf16), picks.astype(bf16), preferred_element_type=f32)
        marks = jnp.where(picks, ranks + 1.0, 0.0)
        marks_sent = jnp.pad(marks, ((0, 0), (0, 128 - experts))).astype(bf16)

        held_a = normed[None, :, :half]
        held_b = jnp.concatenate([normed[:, half:], marks_sent], axis=1)[None]
        for step in range(3):
            masks_a = (Y_STEPS + X_STEPS)[step]
            masks_b = (X_STEPS + Y_STEPS)[step]
            got_a, got_b = swap(held_a, masks_a), swap(held_b, masks_b)
            held_a = jnp.concatenate([held_a, got_a])
            held_b = jnp.concatenate([held_b, got_b])
            if step == 0:
                started = got_a
        last_a, last_b = swap(held_a, X_STEPS[1]), swap(held_b, Y_STEPS[1])
        other_a, other_b = swap(held_a, SIBLING), swap(held_b, SIBLING)

        near = jnp.where(core == 1, 3, 1)
        far = near ^ 2

        def columns(mask):
            return lax.dynamic_slice_in_dim(w_down[layer, 0], (z ^ mask) * part, part, axis=1)

        first = jnp.stack([columns(near), columns(2)])
        first = z_swap(after(first, started), 0)
        second = z_swap(jnp.stack([columns(far), first[1]]), 1)

        own = state.astype(f32) * scale[:, None] * norm_gain[layer][None, :]
        own = own.astype(bf16).astype(f32)
        scores = jnp.dot(own, router[layer], precision=lax.Precision.HIGHEST)
        scores = after(scores, started)
        scores = scores + z_swap(scores, 0)
        scores = scores + z_swap(scores, 1)
        probs = jax.nn.sigmoid(scores)
        picked = jnp.where(picks, probs, 0.0)
        weights = route_scale * picked / jnp.sum(picked, axis=1, keepdims=True)

        def by_chip(table):
            table = table.reshape(rows, chips, 2)
            return jnp.where(core == 1, table[:, :, ::-1], table)

        slot_iota = lax.broadcasted_iota(jnp.int32, (1, 1, 1, capacity), 3).astype(f32) + 1.0
        mixer = jnp.where(by_chip(marks)[..., None] == slot_iota, by_chip(weights)[..., None], 0.0)
        mixer = mixer.reshape(rows, slots)
        mixer = jnp.concatenate(thirds(mixer)[:2], axis=0)

        def products(own, other, first):
            flat = [block.reshape(-1, block.shape[2]) for block in (own, other)]
            result = gate_up(*flat, w_gate, w_up, layer, first, half)
            return result.reshape(2, 2, 4, rows, 2 * units)

        sums_a = products(held_a, other_a, 0)
        sums_b = products(held_b, other_b, half)
        more_a = products(last_a, swap(last_a, SIBLING), 0)
        far_b = swap(last_b, SIBLING)
        more_b = products(last_b, far_b, half)
        sums = jnp.concatenate([sums_a, more_a], axis=1)
        sums = sums + jnp.concatenate([sums_b, more_b], axis=1).swapaxes(1, 2)
        sums = sums.reshape(2 * chips * rows, 2 * units)
        act = (jax.nn.silu(sums[:, :units]) * sums[:, units:]).astype(bf16)

        mark = jnp.stack([jnp.concatenate([held_b, last_b]), jnp.concatenate([other_b, far_b])])
        mark = mark[..., half:].astype(f32)
        mine = lax.broadcasted_iota(jnp.int32, (1, 1, 1, 128), 3) == me
        mark = jnp.sum(jnp.where(mine, mark, 0.0), axis=3).astype(jnp.int32)
        mark = mark.reshape(2, 4, 4, rows).swapaxes(1, 2).reshape(-1)
        place = ((source & 1) ^ core) * (slots // 2) + (source >> 1) * capacity + mark - 1
        place = jnp.where(mark > 0, place, -1)
        taken = lax.broadcasted_iota(jnp.int32, (slots, 1), 0) == place[None, :]
        act = jnp.dot(taken.astype(bf16), act, preferred_element_type=f32).astype(bf16)

        act_near = z_swap(act, 0)
        act_far = z_swap(jnp.stack([act, act_near]), 1)
        out = down_product(z, (act, act_near, act_far), w_down, layer, first, second)
        kept, given = out[: slots // 2], out[slots // 2 :]
        shape = (chips, capacity, part)
        out = jnp.concatenate([kept.reshape(shape), swap(given, SIBLING).reshape(shape)], axis=1)
        groups = [list(range(c, experts, 2)) for c in range(2)]
        returned = lax.all_to_all(
            out, "expert", split_axis=0, concat_axis=0, axis_index_groups=groups
        ).reshape(slots, part)
        mixed = jnp.dot(mixer, returned, preferred_element_type=f32)
        state = (state.astype(f32) + mixed[:rows] + mixed[rows:]).astype(bf16)
    return state


def solution(mesh):
    placed = (
        P("expert", "tensor"),
        P(None, "tensor"),
        P(None, "tensor", None),
        P(None, "expert", None, "tensor"),
        P(None, "expert", None, "tensor"),
        P(None, "expert", "tensor", None),
        P(None, "expert", None),
    )
    return jax.shard_map(
        body, mesh=mesh, in_specs=placed, out_specs=P("expert", "tensor"), check_vma=False
    )
```

```python
import jax
import jax.numpy as jnp
from jax import lax
from jax.experimental import pallas as pl
from jax.experimental.pallas import tpu as pltpu
from jax.sharding import PartitionSpec as P

route_scale = 2.5
bf16, f32 = jnp.bfloat16, jnp.float32

Y_STEPS = ((2, 6), (6, 2))
X_STEPS = ((8, 24), (24, 8))
SIBLING = (1, 1)


def short(values):
    return lax.reduce_precision(values, 8, 7)


def thirds(values):
    high = short(values)
    middle = short(values - high)
    return [part.astype(bf16) for part in (high, middle, values - high - middle)]


def swap(block, masks):
    count = lax.axis_size("expert")
    return lax.ppermute(block, "expert", [(i, i ^ masks[i & 1]) for i in range(count)])


def z_swap(block, mask):
    count = lax.axis_size("tensor")
    return lax.ppermute(block, "tensor", [(i, i ^ mask) for i in range(count)])


def after(block, *others):
    return lax.optimization_barrier((block, *others))[0]


def gate_up_kernel(own_ref, other_ref, gate_ref, up_ref, out_ref):
    units = gate_ref.shape[-1]
    tokens = jnp.concatenate([own_ref[...], other_ref[...]], axis=0)
    gate = jnp.dot(tokens, gate_ref[0, 0], preferred_element_type=f32)
    up = jnp.dot(tokens, up_ref[0, 0], preferred_element_type=f32)

    @pl.when(pl.program_id(0) == 0)
    def _():
        out_ref[:, :units] = gate
        out_ref[:, units:] = up

    @pl.when(pl.program_id(0) > 0)
    def _():
        out_ref[:, :units] += gate
        out_ref[:, units:] += up


def gate_up(own, other, w_gate, w_up, layer, first):
    rows = own.shape[0]
    units = w_gate.shape[-1]
    width = w_gate.shape[2] // 2
    depth = width // 2
    tokens = pl.BlockSpec((rows, depth), lambda k: (0, k))
    weights = pl.BlockSpec((1, 1, depth, units), lambda k: (layer, 0, first // depth + k, 0))
    return pl.pallas_call(
        gate_up_kernel,
        grid=(width // depth,),
        in_specs=[tokens, tokens, weights, weights],
        out_specs=pl.BlockSpec((2 * rows, 2 * units), lambda k: (0, 0)),
        out_shape=jax.ShapeDtypeStruct((2 * rows, 2 * units), f32),
        compiler_params=pltpu.CompilerParams(vmem_limit_bytes=40 << 20),
        cost_estimate=pl.CostEstimate(
            flops=8 * rows * width * units,
            bytes_accessed=4 * (rows + units) * width + 16 * rows * units,
            transcendentals=0,
        ),
    )(own, other, w_gate, w_up)


def down_kernel(z_ref, *refs):
    acts, weights, out_ref = refs[:4], refs[4:-1], refs[-1]
    acts = jnp.concatenate([act[...] for act in acts], axis=1)
    weights = jnp.concatenate([weights[0][0, 0]] + [w[...] for w in weights[1:]], axis=0)
    out_ref[...] = jnp.dot(acts, weights, preferred_element_type=f32).astype(out_ref.dtype)


def down_product(z, acts, slots, w_down, layer, others):
    units = w_down.shape[2]
    part = others[0].shape[-1]
    steps = 2
    columns = part // steps
    act = pl.BlockSpec((slots, units), lambda n, z: (0, 0))
    return pl.pallas_call(
        down_kernel,
        grid_spec=pltpu.PrefetchScalarGridSpec(
            num_scalar_prefetch=1,
            grid=(steps,),
            in_specs=[act] * 4
            + [pl.BlockSpec((1, 1, units, columns), lambda n, z: (layer, 0, 0, z[0] * steps + n))]
            + [pl.BlockSpec((w.shape[0], columns), lambda n, z: (0, n)) for w in others],
            out_specs=pl.BlockSpec((slots, columns), lambda n, z: (0, n)),
        ),
        out_shape=jax.ShapeDtypeStruct((slots, part), bf16),
        compiler_params=pltpu.CompilerParams(vmem_limit_bytes=40 << 20),
        cost_estimate=pl.CostEstimate(
            flops=8 * slots * units * part,
            bytes_accessed=8 * units * (slots + part) + 2 * slots * part,
            transcendentals=0,
        ),
    )(jnp.full((1,), z, jnp.int32), *acts, w_down, *others)


def body(hidden_in, norm_gain, router, w_gate, w_up, w_down, routes):
    rows, part = hidden_in.shape
    layers, width, units = w_gate.shape[0], w_gate.shape[2], w_gate.shape[3]
    experts = router.shape[2]
    capacity = min(rows, 2 * rows * routes.shape[2] // experts)
    slots = experts * capacity
    chips = experts // 2
    half = width // 2
    me = lax.axis_index("expert")
    core = me & 1
    z = lax.axis_index("tensor")

    gains = jnp.stack(thirds(norm_gain), axis=0).reshape(3 * layers, part)
    opening = jnp.concatenate([hidden_in, gains, jnp.zeros((2, part), bf16)], axis=0)
    opening = lax.all_gather(opening, "tensor", axis=1, tiled=True)
    full = opening[:rows]
    gains = opening[rows : rows + 3 * layers].astype(f32).reshape(3, layers, width)
    gains = gains[0] + gains[1] + gains[2]

    bits = jnp.arange(chips, dtype=jnp.int32)
    sources = []
    for c in range(2):
        masks = [Y_STEPS[0][c], Y_STEPS[1][c], X_STEPS[0][c], X_STEPS[1][c]]
        total = jnp.zeros_like(bits)
        for n, mask in enumerate(masks):
            total = total ^ jnp.where(((bits >> n) & 1) == 1, mask, 0)
        sources.append(total)
    own_source = me ^ jnp.where(core == 1, sources[1], sources[0])
    other_source = (me ^ 1) ^ jnp.where(core == 1, sources[0], sources[1])
    source = jnp.concatenate([own_source, other_source])

    expert_iota = lax.broadcasted_iota(jnp.int32, (1, 1, 1, experts), 3)
    picks = jnp.any(routes[..., None] == expert_iota, axis=2)
    earlier = lax.broadcasted_iota(jnp.int32, (rows, rows), 0) >= lax.broadcasted_iota(
        jnp.int32, (rows, rows), 1
    )
    ranks = jnp.einsum("st,lte->lse", earlier.astype(bf16), picks.astype(bf16), preferred_element_type=f32)
    marks = jnp.where(picks, ranks, 0.0)
    marks_sent = jnp.pad(marks, ((0, 0), (0, 0), (0, 128 - experts))).astype(bf16)

    state = hidden_in
    for layer in range(layers):
        if layer:
            full = lax.all_gather(state, "tensor", axis=1, tiled=True)
        values = full.astype(f32)
        scale = lax.rsqrt(jnp.sum(values * values, axis=1) / width + 1e-06)
        normed = (values * scale[:, None] * gains[layer][None, :]).astype(bf16)

        def columns(mask, first, count, *bound):
            column = (after(z, *bound) ^ mask) * part
            block = lax.dynamic_slice(w_down, (layer, 0, first, column), (1, 1, count, part))
            return z_swap(block.reshape(count, part), mask)

        held_a = normed[None, :, :half]
        held_b = jnp.concatenate([normed[:, half:], marks_sent[layer]], axis=1)[None]
        near = [columns(mask, 0, units // 2, normed) for mask in (1, 3)]
        for step in range(3):
            if step == 2:
                held_a, held_b, *near = lax.optimization_barrier((held_a, held_b, *near))
                more = [columns(mask, units // 2, units // 2, held_a, held_b) for mask in (1, 3)]
            got_a = swap(held_a, (Y_STEPS + X_STEPS)[step])
            got_b = swap(held_b, (X_STEPS + Y_STEPS)[step])
            held_a = jnp.concatenate([held_a, got_a])
            held_b = jnp.concatenate([held_b, got_b])
        held_a, held_b, *more = lax.optimization_barrier((held_a, held_b, *more))
        far = columns(2, 0, units, held_a, held_b)
        last_a, last_b = swap(held_a, X_STEPS[1]), swap(held_b, Y_STEPS[1])
        other_a, other_b = swap(held_a, SIBLING), swap(held_b, SIBLING)

        def products(own, other, first):
            flat = [block.reshape(-1, block.shape[2]) for block in (own, other)]
            return gate_up(*flat, w_gate, w_up, layer, first)

        sums_a = products(held_a, other_a, 0)
        sums_b = products(held_b, other_b, half)
        last_a, last_b, sums_a, sums_b, far = lax.optimization_barrier(
            (last_a, last_b, sums_a, sums_b, far)
        )
        last_other_a, last_other_b = swap(last_a, SIBLING), swap(last_b, SIBLING)
        more_a = products(last_a, last_other_a, 0)
        more_b = products(last_b, last_other_b, half)

        mine = lax.broadcasted_iota(jnp.int32, (1, 1, 128), 2) == me
        mark = [
            jnp.sum(jnp.where(mine, block[:, :, half:].astype(f32), 0.0), axis=2)
            for block in (held_b, last_b, other_b, last_other_b)
        ]
        mark = jnp.concatenate(mark).reshape(2, 4, 4, rows).swapaxes(1, 2).reshape(2 * chips, rows)
        mark = mark.astype(jnp.int32)
        slot = jnp.where(mark > 0, source[:, None] * capacity + mark - 1, -1).reshape(1, -1)
        taken = (lax.broadcasted_iota(jnp.int32, (slots, 1), 0) == slot).astype(bf16)

        def in_order(held, last):
            blocks = (2, 2, 4, rows, 2 * units)
            return jnp.concatenate([held.reshape(blocks), last.reshape(blocks)], axis=1)

        sums = in_order(sums_a, more_a) + in_order(sums_b, more_b).swapaxes(1, 2)
        sums = sums.reshape(2 * chips * rows, 2 * units)
        act = (jax.nn.silu(sums[:, :units]) * sums[:, units:]).astype(bf16)
        act = jnp.dot(taken, act, preferred_element_type=f32).astype(bf16)


        own = state.astype(f32) * scale[:, None] * norm_gain[layer][None, :]
        own = own.astype(bf16).astype(f32)
        scores = jnp.dot(own, router[layer], precision=lax.Precision.HIGHEST)
        scores = jnp.pad(jnp.concatenate(thirds(scores), axis=1), ((0, 0), (0, units - 3 * experts)))
        act = jnp.concatenate([act, scores], axis=0)
        acts = [act] + [z_swap(act, mask) for mask in (1, 3, 2)]
        scores = sum(block[slots:].astype(f32) for block in acts)
        scores = sum(scores[:, experts * n : experts * (n + 1)] for n in range(3))
        others = [near[0], more[0], near[1], more[1], far]
        out = down_product(z, acts, slots, w_down, layer, others)
        probs = jax.nn.sigmoid(scores)
        picked = jnp.where(picks[layer], probs, 0.0)
        weights = route_scale * picked / jnp.sum(picked, axis=1, keepdims=True)
        slot_iota = lax.broadcasted_iota(jnp.int32, (1, 1, capacity), 2).astype(f32) + 1.0
        mixer = jnp.where(marks[layer][:, :, None] == slot_iota, weights[:, :, None], 0.0)
        mixer = jnp.concatenate(thirds(mixer.reshape(rows, slots))[:2], axis=0)

        returned = lax.all_to_all(
            out.reshape(experts, capacity, part), "expert", split_axis=0, concat_axis=0
        ).reshape(slots, part)
        mixed = jnp.dot(mixer, returned, preferred_element_type=f32)
        state = (state.astype(f32) + mixed[:rows] + mixed[rows:]).astype(bf16)
    return state


def solution(mesh):
    placed = (
        P("expert", "tensor"),
        P(None, "tensor"),
        P(None, "tensor", None),
        P(None, "expert", None, "tensor"),
        P(None, "expert", None, "tensor"),
        P(None, "expert", "tensor", None),
        P(None, "expert", None),
    )
    return jax.shard_map(
        body, mesh=mesh, in_specs=placed, out_specs=P("expert", "tensor"), check_vma=False
    )
```

```python
import functools

import jax
import jax.numpy as jnp
from jax import lax
from jax.experimental import pallas as pl
from jax.experimental.pallas import tpu as pltpu
from jax.sharding import PartitionSpec as P

route_scale = 2.5
bf16, f32 = jnp.bfloat16, jnp.float32

Y_STEPS = ((2, 6), (6, 2))
X_STEPS = ((8, 24), (24, 8))
SIBLING = (1, 1)
ORDER = (0, 1, 3, 2)
VMEM = 24 << 20


def short(values):
    return lax.reduce_precision(values, 8, 7)


def thirds(values):
    high = short(values)
    middle = short(values - high)
    return [part.astype(bf16) for part in (high, middle, values - high - middle)]


def swap(block, masks):
    count = lax.axis_size("expert")
    return lax.ppermute(block, "expert", [(i, i ^ masks[i & 1]) for i in range(count)])


def z_swap(block, mask):
    count = lax.axis_size("tensor")
    return lax.ppermute(block, "tensor", [(i, i ^ mask) for i in range(count)])


def after(block, *others):
    return lax.optimization_barrier((block, *others))[0]


def gate_up_kernel(layer, first, z_ref, own_ref, other_ref, gate_ref, up_ref, out_ref, held, sems):
    depth, units = held.shape[2:]
    copies = []
    for k in range(2):
        start = pl.multiple_of((z_ref[0] ^ (k ^ first)) * depth, depth)
        for n, weights in enumerate((gate_ref, up_ref)):
            source = weights.at[layer, 0, pl.ds(start, depth)]
            copies.append(pltpu.make_async_copy(source, held.at[k, n], sems.at[k, n]))
    for copy in copies:
        copy.start()
    for k in range(2):
        features = slice(k * depth, (k + 1) * depth)
        tokens = jnp.concatenate([own_ref[:, features], other_ref[:, features]], axis=0)
        for n in range(2):
            copies[2 * k + n].wait()
            product = jnp.dot(tokens, held[k, n], preferred_element_type=f32)
            if k:
                product += out_ref[:, n * units : (n + 1) * units]
            out_ref[:, n * units : (n + 1) * units] = product


def gate_up(z, own, other, w_gate, w_up, layer, first):
    rows, units = own.shape[0], w_gate.shape[-1]
    depth = w_gate.shape[2] // 4
    near, far = pl.BlockSpec(memory_space=pltpu.VMEM), pl.BlockSpec(memory_space=pltpu.HBM)
    return pl.pallas_call(
        functools.partial(gate_up_kernel, layer, first),
        in_specs=[pl.BlockSpec(memory_space=pltpu.SMEM), near, near, far, far],
        out_specs=near,
        out_shape=jax.ShapeDtypeStruct((2 * rows, 2 * units), f32),
        scratch_shapes=[
            pltpu.VMEM((2, 2, depth, units), bf16),
            pltpu.SemaphoreType.DMA((2, 2)),
        ],
        compiler_params=pltpu.CompilerParams(vmem_limit_bytes=VMEM),
        cost_estimate=pl.CostEstimate(
            flops=16 * rows * depth * units,
            bytes_accessed=8 * (rows + units) * depth + 16 * rows * units,
            transcendentals=0,
        ),
    )(jnp.full((1,), z, jnp.int32), own, other, w_gate, w_up)


def down_kernel(layer, slots, capacity, padded, z_ref, *refs):
    acts, down_ref, others, out_ref, own, sem = refs[:4], refs[4], refs[5:-3], *refs[-3:]
    units, part = own.shape
    column = pl.multiple_of(z_ref[0] * part, part)
    copy = pltpu.make_async_copy(down_ref.at[layer, 0, :, pl.ds(column, part)], own, sem)
    copy.start()
    row = lax.broadcasted_iota(jnp.int32, (slots // capacity * padded, slots), 0)
    slot = lax.broadcasted_iota(jnp.int32, row.shape, 1)
    place = row % padded
    here = (place < capacity) & (row // padded * capacity + place == slot)
    joined = jnp.concatenate([act[:slots] for act in acts], axis=1)
    joined = jnp.dot(here.astype(bf16), joined, preferred_element_type=f32).astype(bf16)
    copy.wait()
    half = part // 2
    for n in range(2):
        columns = slice(n * half, (n + 1) * half)
        weights = jnp.concatenate([own[:, columns]] + [w[:, columns] for w in others], axis=0)
        out_ref[:, columns] = jnp.dot(joined, weights, preferred_element_type=f32).astype(bf16)


def down_product(z, acts, slots, capacity, padded, w_down, layer, others):
    units = w_down.shape[2]
    part = others[0].shape[-1]
    rows = slots // capacity * padded
    near, far = pl.BlockSpec(memory_space=pltpu.VMEM), pl.BlockSpec(memory_space=pltpu.HBM)
    return pl.pallas_call(
        functools.partial(down_kernel, layer, slots, capacity, padded),
        in_specs=[pl.BlockSpec(memory_space=pltpu.SMEM)] + [near] * 4 + [far] + [near] * len(others),
        out_specs=near,
        out_shape=jax.ShapeDtypeStruct((rows, part), bf16),
        scratch_shapes=[pltpu.VMEM((units, part), bf16), pltpu.SemaphoreType.DMA],
        compiler_params=pltpu.CompilerParams(vmem_limit_bytes=VMEM),
        cost_estimate=pl.CostEstimate(
            flops=8 * rows * units * (part + slots),
            bytes_accessed=8 * units * (slots + part) + 2 * rows * part,
            transcendentals=0,
        ),
    )(jnp.full((1,), z, jnp.int32), *acts, w_down, *others)


def body(hidden_in, norm_gain, router, w_gate, w_up, w_down, routes):
    rows, part = hidden_in.shape
    layers, width, units = w_gate.shape[0], w_gate.shape[2], w_gate.shape[3]
    experts = router.shape[2]
    capacity = min(rows, 2 * rows * routes.shape[2] // experts)
    slots = experts * capacity
    padded = -(-capacity // 16) * 16
    chips = experts // 2
    half = width // 2
    me = lax.axis_index("expert")
    core = me & 1
    z = lax.axis_index("tensor")

    bits = jnp.arange(chips, dtype=jnp.int32)
    sources = []
    for c in range(2):
        masks = [Y_STEPS[0][c], Y_STEPS[1][c], X_STEPS[0][c], X_STEPS[1][c]]
        total = jnp.zeros_like(bits)
        for n, mask in enumerate(masks):
            total = total ^ jnp.where(((bits >> n) & 1) == 1, mask, 0)
        sources.append(total)
    own_source = me ^ jnp.where(core == 1, sources[1], sources[0])
    other_source = (me ^ 1) ^ jnp.where(core == 1, sources[0], sources[1])
    source = jnp.concatenate([own_source, other_source])

    expert_iota = lax.broadcasted_iota(jnp.int32, (1, 1, 1, experts), 3)
    picks = jnp.any(routes[..., None] == expert_iota, axis=2)
    earlier = lax.broadcasted_iota(jnp.int32, (rows, rows), 0) >= lax.broadcasted_iota(
        jnp.int32, (rows, rows), 1
    )
    ranks = jnp.einsum("st,lte->lse", earlier.astype(bf16), picks.astype(bf16), preferred_element_type=f32)
    marks = jnp.where(picks, ranks, 0.0)
    marks_sent = jnp.pad(marks, ((0, 0), (0, 0), (0, 128 - experts))).astype(bf16)

    def spread(block):
        return [block] + [z_swap(block, mask) for mask in ORDER[1:]]

    def columns(layer, mask, first, count, *bound):
        column = (after(z, *bound) ^ mask) * part
        block = lax.dynamic_slice(w_down, (layer, 0, first, column), (1, 1, count, part))
        return block.reshape(count, part)

    def reshard(layer, mask, first, count, *bound):
        return z_swap(columns(layer, mask, first, count, *bound), mask)

    state = hidden_in
    gains = jnp.stack(thirds(norm_gain), axis=0).reshape(3 * layers, part)
    gains = spread(jnp.pad(gains, ((0, 8 - 3 * layers), (0, 0))))
    gains = [
        block[: 3 * layers].astype(f32).reshape(3, layers, part).sum(axis=0) for block in gains
    ]
    for layer in range(layers):
        blocks = [block.astype(f32) for block in spread(state)]
        scale = sum(jnp.sum(block * block, axis=1) for block in blocks)
        scale = lax.rsqrt(scale / width + 1e-06)
        normed = [
            (block * scale[:, None] * gain[layer][None, :]).astype(bf16)
            for block, gain in zip(blocks, gains)
        ]

        held_a = jnp.concatenate(normed[:2], axis=1)[None]
        held_b = jnp.concatenate(normed[2:] + [marks_sent[layer]], axis=1)[None]
        if layer == 0:
            near = [reshard(layer, mask, 0, units // 2, held_a) for mask in ORDER[1:3]]
        far = columns(layer, 2, 0, units, held_a)
        for step in range(3):
            if layer == 0 and step == 2:
                held_a, held_b, *near = lax.optimization_barrier((held_a, held_b, *near))
                more = [reshard(layer, mask, units // 2, units // 2, held_a, held_b) for mask in ORDER[1:3]]
            got_a = swap(held_a, (Y_STEPS + X_STEPS)[step])
            got_b = swap(held_b, (X_STEPS + Y_STEPS)[step])
            held_a = jnp.concatenate([held_a, got_a])
            held_b = jnp.concatenate([held_b, got_b])
        if layer == 0:
            held_a, held_b, far, *more = lax.optimization_barrier((held_a, held_b, far, *more))
            near = [near[0], more[0], near[1], more[1]]
        else:
            held_a, held_b, far = lax.optimization_barrier((held_a, held_b, far))
        far = z_swap(far, 2)
        last_a, last_b = swap(held_a, X_STEPS[1]), swap(held_b, Y_STEPS[1])
        other_a, other_b = swap(held_a, SIBLING), swap(held_b, SIBLING)

        def products(own, other, first):
            flat = [block.reshape(-1, block.shape[2]) for block in (own, other)]
            return gate_up(z, *flat, w_gate, w_up, layer, first)

        sums_a = products(held_a, other_a, 0)
        sums_b = products(held_b, other_b, 3)
        last_a, last_b, sums_a, sums_b, far = lax.optimization_barrier(
            (last_a, last_b, sums_a, sums_b, far)
        )
        last_other_a, last_other_b = swap(last_a, SIBLING), swap(last_b, SIBLING)
        more_a = products(last_a, last_other_a, 0)
        more_b = products(last_b, last_other_b, 3)

        mine = lax.broadcasted_iota(jnp.int32, (1, 1, 128), 2) == me
        mark = [
            jnp.sum(jnp.where(mine, block[:, :, half:].astype(f32), 0.0), axis=2)
            for block in (held_b, last_b, other_b, last_other_b)
        ]
        mark = jnp.concatenate(mark).reshape(2, 4, 4, rows).swapaxes(1, 2).reshape(2 * chips, rows)
        mark = mark.astype(jnp.int32)
        slot = jnp.where(mark > 0, source[:, None] * capacity + mark - 1, -1).reshape(1, -1)
        taken = (lax.broadcasted_iota(jnp.int32, (slots, 1), 0) == slot).astype(bf16)

        def in_order(held, last):
            blocks = (2, 2, 4, rows, 2 * units)
            return jnp.concatenate([held.reshape(blocks), last.reshape(blocks)], axis=1)

        sums = in_order(sums_a, more_a) + in_order(sums_b, more_b).swapaxes(1, 2)
        sums = sums.reshape(2 * chips * rows, 2 * units)
        act = (jax.nn.silu(sums[:, :units]) * sums[:, units:]).astype(bf16)
        act = jnp.dot(taken, act, preferred_element_type=f32).astype(bf16)


        own = state.astype(f32) * scale[:, None] * norm_gain[layer][None, :]
        own = own.astype(bf16).astype(f32)
        scores = jnp.dot(own, router[layer], precision=lax.Precision.HIGHEST)
        scores = jnp.pad(jnp.concatenate(thirds(scores), axis=1), ((0, 0), (0, units - 3 * experts)))
        act = jnp.concatenate([act, scores], axis=0)
        acts = spread(act)
        scores = sum(block[slots:].astype(f32) for block in acts)
        scores = sum(scores[:, experts * n : experts * (n + 1)] for n in range(3))
        out = down_product(z, acts, slots, capacity, padded, w_down, layer, near + [far])
        probs = jax.nn.sigmoid(scores)
        picked = jnp.where(picks[layer], probs, 0.0)
        weights = route_scale * picked / jnp.sum(picked, axis=1, keepdims=True)
        slot_iota = lax.broadcasted_iota(jnp.int32, (1, 1, padded), 2).astype(f32) + 1.0
        mixer = jnp.where(marks[layer][:, :, None] == slot_iota, weights[:, :, None], 0.0)
        mixer = jnp.concatenate(thirds(mixer.reshape(rows, experts * padded))[:2], axis=0)

        returned = lax.all_to_all(
            out.reshape(experts, padded, part), "expert", split_axis=0, concat_axis=0
        ).reshape(experts * padded, part)
        if layer + 1 < layers:
            near = [reshard(layer + 1, mask, 0, units, out) for mask in ORDER[1:3]]
            returned, *near = lax.optimization_barrier((returned, *near))
        mixed = jnp.dot(mixer, returned, preferred_element_type=f32)
        state = (state.astype(f32) + mixed[:rows] + mixed[rows:]).astype(bf16)
    return state


def solution(mesh):
    placed = (
        P("expert", "tensor"),
        P(None, "tensor"),
        P(None, "tensor", None),
        P(None, "expert", None, "tensor"),
        P(None, "expert", None, "tensor"),
        P(None, "expert", "tensor", None),
        P(None, "expert", None),
    )
    return jax.shard_map(
        body, mesh=mesh, in_specs=placed, out_specs=P("expert", "tensor"), check_vma=False
    )
```

```python
import functools

import jax
import jax.numpy as jnp
from jax import lax
from jax.experimental import pallas as pl
from jax.experimental.pallas import tpu as pltpu
from jax.sharding import PartitionSpec as P

route_scale = 2.5
bf16, f32 = jnp.bfloat16, jnp.float32

ORDER = (0, 1, 3, 2)


def short(values):
    return lax.reduce_precision(values, 8, 7)


def thirds(values):
    high = short(values)
    middle = short(values - high)
    return [part.astype(bf16) for part in (high, middle, values - high - middle)]


def z_swap(block, mask):
    count = lax.axis_size("tensor")
    return lax.ppermute(block, "tensor", [(i, i ^ mask) for i in range(count)])


def after(block, *others):
    return lax.optimization_barrier((block, *others))[0]


def gate_up_kernel(z_ref, tokens_ref, gate_ref, up_ref, act_ref, gate_sum, up_sum):
    step = pl.program_id(0)
    gate = jnp.dot(tokens_ref[...], gate_ref[0, 0], preferred_element_type=f32)
    up = jnp.dot(tokens_ref[...], up_ref[0, 0], preferred_element_type=f32)

    @pl.when(step == 0)
    def _():
        gate_sum[...] = gate
        up_sum[...] = up

    @pl.when(step > 0)
    def _():
        gate_sum[...] += gate
        up_sum[...] += up

    @pl.when(step == pl.num_programs(0) - 1)
    def _():
        gate = gate_sum[...]
        act_ref[...] = (gate / (1.0 + jnp.exp(-gate)) * up_sum[...]).astype(act_ref.dtype)


def gate_up(z, tokens, w_gate, w_up, layer):
    rows, units = tokens.shape[0], w_gate.shape[-1]
    depth = w_gate.shape[2] // 4
    weights = pl.BlockSpec((1, 1, depth, units), lambda k, z: (layer, 0, z[0] ^ k ^ (k >> 1), 0))
    return pl.pallas_call(
        gate_up_kernel,
        grid_spec=pltpu.PrefetchScalarGridSpec(
            num_scalar_prefetch=1,
            grid=(4,),
            in_specs=[pl.BlockSpec((rows, depth), lambda k, z: (0, k)), weights, weights],
            out_specs=pl.BlockSpec((rows, units), lambda k, z: (0, 0)),
            scratch_shapes=[pltpu.VMEM((rows, units), f32)] * 2,
        ),
        out_shape=jax.ShapeDtypeStruct((rows, units), bf16),
        cost_estimate=pl.CostEstimate(
            flops=16 * rows * depth * units,
            bytes_accessed=8 * (rows + 2 * units) * depth + 2 * rows * units,
            transcendentals=rows * units,
        ),
    )(jnp.full((1,), z, jnp.int32), tokens, w_gate, w_up)


def down_kernel(capacity, padded, z_ref, *refs):
    acts, weights, out_ref, held = refs[:4], refs[4:-2], refs[-2], refs[-1]

    @pl.when(pl.program_id(0) == 0)
    def _():
        slots = acts[0].shape[0]
        row = lax.broadcasted_iota(jnp.int32, (slots // capacity * padded, slots), 0)
        slot = lax.broadcasted_iota(jnp.int32, row.shape, 1)
        place = row % padded
        here = (place < capacity) & (row // padded * capacity + place == slot)
        joined = jnp.concatenate([act[...] for act in acts], axis=1)
        spread = jnp.dot(here.astype(bf16), joined, preferred_element_type=f32)
        held[...] = spread.astype(bf16)

    weights = jnp.concatenate([weights[0][0, 0]] + [w[...] for w in weights[1:]], axis=0)
    out_ref[...] = jnp.dot(held[...], weights, preferred_element_type=f32).astype(out_ref.dtype)


def down_product(z, acts, slots, capacity, padded, w_down, layer, others):
    units = w_down.shape[2]
    part = others[0].shape[-1]
    rows = slots // capacity * padded
    steps = 2
    columns = part // steps
    act = pl.BlockSpec((slots, units), lambda n, z: (0, 0))
    return pl.pallas_call(
        functools.partial(down_kernel, capacity, padded),
        grid_spec=pltpu.PrefetchScalarGridSpec(
            num_scalar_prefetch=1,
            grid=(steps,),
            in_specs=[act] * 4
            + [pl.BlockSpec((1, 1, units, columns), lambda n, z: (layer, 0, 0, z[0] * steps + n))]
            + [pl.BlockSpec((w.shape[0], columns), lambda n, z: (0, n)) for w in others],
            out_specs=pl.BlockSpec((rows, columns), lambda n, z: (0, n)),
            scratch_shapes=[pltpu.VMEM((rows, 4 * units), bf16)],
        ),
        out_shape=jax.ShapeDtypeStruct((rows, part), bf16),
        cost_estimate=pl.CostEstimate(
            flops=8 * rows * units * (part + slots),
            bytes_accessed=8 * units * (slots + part) + 2 * rows * part,
            transcendentals=0,
        ),
    )(jnp.full((1,), z, jnp.int32), *acts, w_down, *others)


def body(hidden_in, norm_gain, router, w_gate, w_up, w_down, routes):
    rows, part = hidden_in.shape
    layers, width, units = w_gate.shape[0], w_gate.shape[2], w_gate.shape[3]
    experts = router.shape[2]
    capacity = min(rows, 2 * rows * routes.shape[2] // experts)
    slots = experts * capacity
    padded = -(-capacity // 16) * 16
    me = lax.axis_index("expert")
    z = lax.axis_index("tensor")

    expert_iota = lax.broadcasted_iota(jnp.int32, (1, 1, 1, experts), 3)
    picks = jnp.any(routes[..., None] == expert_iota, axis=2)
    earlier = lax.broadcasted_iota(jnp.int32, (rows, rows), 0) >= lax.broadcasted_iota(
        jnp.int32, (rows, rows), 1
    )
    ranks = jnp.einsum("st,lte->lse", earlier.astype(bf16), picks.astype(bf16), preferred_element_type=f32)
    marks = jnp.where(picks, ranks, 0.0)
    marks_sent = jnp.pad(marks, ((0, 0), (0, 0), (0, 128 - experts))).astype(bf16)

    def spread(block):
        return [block] + [z_swap(block, mask) for mask in ORDER[1:]]

    def columns(layer, mask, first, count, *bound):
        column = (after(z, *bound) ^ mask) * part
        block = lax.dynamic_slice(w_down, (layer, 0, first, column), (1, 1, count, part))
        return z_swap(block.reshape(count, part), mask)

    state = hidden_in
    gains = jnp.stack(thirds(norm_gain), axis=0).reshape(3 * layers, part)
    gains = spread(jnp.pad(gains, ((0, 8 - 3 * layers), (0, 0))))
    gains = [
        block[: 3 * layers].astype(f32).reshape(3, layers, part).sum(axis=0) for block in gains
    ]
    for layer in range(layers):
        blocks = [block.astype(f32) for block in spread(state)]
        scale = sum(jnp.sum(block * block, axis=1) for block in blocks)
        scale = lax.rsqrt(scale / width + 1e-06)
        normed = [
            (block * scale[:, None] * gain[layer][None, :]).astype(bf16)
            for block, gain in zip(blocks, gains)
        ]

        sent = jnp.concatenate(normed + [marks_sent[layer]], axis=1)
        arrived = lax.all_gather(sent, "expert", axis=0, tiled=True)
        others = [columns(layer, mask, 0, units, sent) for mask in ORDER[1:]]
        arrived, *others = lax.optimization_barrier((arrived, *others))
        act = gate_up(z, arrived, w_gate, w_up, layer)

        mine = lax.broadcasted_iota(jnp.int32, (1, 128), 1) == me
        mark = jnp.sum(jnp.where(mine, arrived[:, width:].astype(f32), 0.0), axis=1).astype(jnp.int32)
        source = lax.broadcasted_iota(jnp.int32, (experts, rows), 0).reshape(-1)
        slot = jnp.where(mark > 0, source * capacity + mark - 1, -1)[None, :]
        taken = (lax.broadcasted_iota(jnp.int32, (slots, 1), 0) == slot).astype(bf16)

        act = jnp.dot(taken, act, preferred_element_type=f32).astype(bf16)

        own = state.astype(f32) * scale[:, None] * norm_gain[layer][None, :]
        own = own.astype(bf16).astype(f32)
        scores = jnp.dot(own, router[layer], precision=lax.Precision.HIGHEST)
        scores = jnp.pad(jnp.concatenate(thirds(scores), axis=1), ((0, 0), (0, units - 3 * experts)))
        act = jnp.concatenate([act, scores], axis=0)
        acts = spread(act)
        scores = sum(block[slots:].astype(f32) for block in acts)
        scores = sum(scores[:, experts * n : experts * (n + 1)] for n in range(3))
        out = down_product(z, acts, slots, capacity, padded, w_down, layer, others)
        probs = jax.nn.sigmoid(scores)
        picked = jnp.where(picks[layer], probs, 0.0)
        weights = route_scale * picked / jnp.sum(picked, axis=1, keepdims=True)
        slot_iota = lax.broadcasted_iota(jnp.int32, (1, 1, padded), 2).astype(f32) + 1.0
        mixer = jnp.where(marks[layer][:, :, None] == slot_iota, weights[:, :, None], 0.0)
        mixer = jnp.concatenate(thirds(mixer.reshape(rows, experts * padded))[:2], axis=0)

        returned = lax.all_to_all(
            out.reshape(experts, padded, part), "expert", split_axis=0, concat_axis=0
        ).reshape(experts * padded, part)
        mixed = jnp.dot(mixer, returned, preferred_element_type=f32)
        state = (state.astype(f32) + mixed[:rows] + mixed[rows:]).astype(bf16)
    return state


def solution(mesh):
    placed = (
        P("expert", "tensor"),
        P(None, "tensor"),
        P(None, "tensor", None),
        P(None, "expert", None, "tensor"),
        P(None, "expert", None, "tensor"),
        P(None, "expert", "tensor", None),
        P(None, "expert", None),
    )
    return jax.shard_map(
        body, mesh=mesh, in_specs=placed, out_specs=P("expert", "tensor"), check_vma=False
    )
```

```python
import functools

import jax
import jax.numpy as jnp
from jax import lax
from jax.experimental import pallas as pl
from jax.experimental.pallas import tpu as pltpu
from jax.sharding import PartitionSpec as P

route_scale = 2.5
bf16, f32 = jnp.bfloat16, jnp.float32

Y_STEPS = ((2, 6), (6, 2))
X_STEPS = ((8, 24), (24, 8))
SIBLING = (1, 1)
ORDER = (0, 1, 3, 2)


def short(values):
    return lax.reduce_precision(values, 8, 7)


def thirds(values):
    high = short(values)
    middle = short(values - high)
    return [part.astype(bf16) for part in (high, middle, values - high - middle)]


def swap(block, masks):
    count = lax.axis_size("expert")
    return lax.ppermute(block, "expert", [(i, i ^ masks[i & 1]) for i in range(count)])


def z_swap(block, mask):
    count = lax.axis_size("tensor")
    return lax.ppermute(block, "tensor", [(i, i ^ mask) for i in range(count)])


def after(block, *others):
    return lax.optimization_barrier((block, *others))[0]


def first_kernel(z_ref, t0, t1, t2, t3, gate_ref, up_ref, out_ref):
    units = gate_ref.shape[-1]
    tokens = jnp.concatenate([t0[...], t1[...], t2[...], t3[...]], axis=0)
    out_ref[:, :units] = jnp.dot(tokens, gate_ref[0, 0], preferred_element_type=f32)
    out_ref[:, units:] = jnp.dot(tokens, up_ref[0, 0], preferred_element_type=f32)


def first_products(z, tokens, w_gate, w_up, layer, mask):
    rows, units = tokens[0].shape[0], w_gate.shape[-1]
    depth = w_gate.shape[2] // 4
    weights = pl.BlockSpec((1, 1, depth, units), lambda k, z: (layer, 0, z[0] ^ mask, 0))
    return pl.pallas_call(
        first_kernel,
        grid_spec=pltpu.PrefetchScalarGridSpec(
            num_scalar_prefetch=1,
            grid=(1,),
            in_specs=[pl.BlockSpec((rows, depth), lambda k, z: (0, 0))] * 4 + [weights, weights],
            out_specs=pl.BlockSpec((4 * rows, 2 * units), lambda k, z: (0, 0)),
        ),
        out_shape=jax.ShapeDtypeStruct((4 * rows, 2 * units), f32),
        cost_estimate=pl.CostEstimate(
            flops=16 * rows * depth * units,
            bytes_accessed=8 * rows * depth + 4 * units * depth + 32 * rows * units,
            transcendentals=0,
        ),
    )(jnp.full((1,), z, jnp.int32), *tokens, w_gate, w_up)


def gate_up_kernel(rows, z_ref, places_ref, tokens_ref, gate_ref, up_ref, a_ref, b_ref, act_ref, held):
    units = gate_ref.shape[-1]
    step = pl.program_id(0)

    @pl.when(step == 0)
    def _():
        for block in range(held.shape[0] // rows):
            first = pl.multiple_of(places_ref[0, block] * rows, rows)
            second = pl.multiple_of(places_ref[1, block] * rows, rows)
            held[block * rows : (block + 1) * rows] = (
                a_ref[pl.ds(first, rows)] + b_ref[pl.ds(second, rows)]
            )

    held[:, :units] += jnp.dot(tokens_ref[...], gate_ref[0, 0], preferred_element_type=f32)
    held[:, units:] += jnp.dot(tokens_ref[...], up_ref[0, 0], preferred_element_type=f32)

    @pl.when(step == pl.num_programs(0) - 1)
    def _():
        gate = held[:, :units]
        act_ref[...] = (gate / (1.0 + jnp.exp(-gate)) * held[:, units:]).astype(act_ref.dtype)


def gate_up(z, places, tokens, w_gate, w_up, layer, sums_a, sums_b, rows):
    total, units = tokens.shape[0], w_gate.shape[-1]
    depth = w_gate.shape[2] // 4
    weights = pl.BlockSpec((1, 1, depth, units), lambda k, z, p: (layer, 0, z[0] ^ k, 0))
    sums = pl.BlockSpec((total, 2 * units), lambda k, z, p: (0, 0))
    return pl.pallas_call(
        functools.partial(gate_up_kernel, rows),
        grid_spec=pltpu.PrefetchScalarGridSpec(
            num_scalar_prefetch=2,
            grid=(2,),
            in_specs=[
                pl.BlockSpec((total, depth), lambda k, z, p: (0, k)),
                weights,
                weights,
                sums,
                sums,
            ],
            out_specs=pl.BlockSpec((total, units), lambda k, z, p: (0, 0)),
            scratch_shapes=[pltpu.VMEM((total, 2 * units), f32)],
        ),
        out_shape=jax.ShapeDtypeStruct((total, units), bf16),
        compiler_params=pltpu.CompilerParams(vmem_limit_bytes=48 << 20),
        cost_estimate=pl.CostEstimate(
            flops=8 * total * depth * units,
            bytes_accessed=4 * (total + 2 * units) * depth + 18 * total * units,
            transcendentals=total * units,
        ),
    )(jnp.full((1,), z, jnp.int32), places, tokens, w_gate, w_up, sums_a, sums_b)


def down_kernel(capacity, padded, z_ref, *refs):
    acts, weights, out_ref = refs[:4], refs[4:-1], refs[-1]
    acts = jnp.concatenate([act[...] for act in acts], axis=1)
    weights = jnp.concatenate([weights[0][0, 0]] + [w[...] for w in weights[1:]], axis=0)
    product = jnp.dot(acts, weights, preferred_element_type=f32)
    blank = jnp.zeros((padded - capacity, product.shape[1]), f32)
    for block in range(product.shape[0] // capacity):
        here = product[block * capacity : (block + 1) * capacity]
        here = jnp.concatenate([here, blank], axis=0).astype(out_ref.dtype)
        out_ref[block * padded : (block + 1) * padded] = here


def down_product(z, acts, slots, capacity, padded, w_down, layer, others):
    units = w_down.shape[2]
    part = others[0].shape[-1]
    rows = slots // capacity * padded
    steps = 2
    columns = part // steps
    act = pl.BlockSpec((slots, units), lambda n, z: (0, 0))
    return pl.pallas_call(
        functools.partial(down_kernel, capacity, padded),
        grid_spec=pltpu.PrefetchScalarGridSpec(
            num_scalar_prefetch=1,
            grid=(steps,),
            in_specs=[act] * 4
            + [pl.BlockSpec((1, 1, units, columns), lambda n, z: (layer, 0, 0, z[0] * steps + n))]
            + [pl.BlockSpec((w.shape[0], columns), lambda n, z: (0, n)) for w in others],
            out_specs=pl.BlockSpec((rows, columns), lambda n, z: (0, n)),
        ),
        out_shape=jax.ShapeDtypeStruct((rows, part), bf16),
        cost_estimate=pl.CostEstimate(
            flops=8 * slots * units * part,
            bytes_accessed=8 * units * (slots + part) + 2 * rows * part,
            transcendentals=0,
        ),
    )(jnp.full((1,), z, jnp.int32), *acts, w_down, *others)


def body(hidden_in, norm_gain, router, w_gate, w_up, w_down, routes):
    rows, part = hidden_in.shape
    layers, width, units = w_gate.shape[0], w_gate.shape[2], w_gate.shape[3]
    experts = router.shape[2]
    capacity = min(rows, 2 * rows * routes.shape[2] // experts)
    slots = experts * capacity
    padded = -(-capacity // 16) * 16
    me = lax.axis_index("expert")
    z = lax.axis_index("tensor")

    away = lax.broadcasted_iota(jnp.int32, (experts,), 0) ^ me
    odd = ((away ^ me) & 1) == 1

    def turns(distance):
        low, high = (distance & 1) ^ (distance >> 1), distance >> 1
        return jnp.where(odd, high, low) + 2 * jnp.where(odd, low, high)

    along_y, along_x = turns((away >> 1) & 3), turns(away >> 3)
    other = (away & 1) * (experts // 2)
    places = jnp.stack([other + along_y + 4 * along_x, other + along_x + 4 * along_y])
    in_place = places[1][:, None] == lax.broadcasted_iota(jnp.int32, (1, experts), 1)
    in_place = in_place.astype(bf16)

    expert_iota = lax.broadcasted_iota(jnp.int32, (1, 1, 1, experts), 3)
    picks = jnp.any(routes[..., None] == expert_iota, axis=2)
    earlier = lax.broadcasted_iota(jnp.int32, (rows, rows), 0) >= lax.broadcasted_iota(
        jnp.int32, (rows, rows), 1
    )
    ranks = jnp.einsum("st,lte->lse", earlier.astype(bf16), picks.astype(bf16), preferred_element_type=f32)
    marks = jnp.where(picks, ranks, 0.0)
    marks_sent = jnp.pad(marks, ((0, 0), (0, 0), (0, 128 - experts))).astype(bf16)

    def spread(block):
        return [block] + [z_swap(block, mask) for mask in ORDER[1:]]

    def columns(layer, mask, first, count, *bound):
        column = (after(z, *bound) ^ mask) * part
        block = lax.dynamic_slice(w_down, (layer, 0, first, column), (1, 1, count, part))
        return z_swap(block.reshape(count, part), mask)

    state = hidden_in
    gains = jnp.stack(thirds(norm_gain), axis=0).reshape(3 * layers, part)
    gains = spread(jnp.pad(gains, ((0, 8 - 3 * layers), (0, 0))))
    gains = [
        block[: 3 * layers].astype(f32).reshape(3, layers, part).sum(axis=0) for block in gains
    ]
    for layer in range(layers):
        blocks = [block.astype(f32) for block in spread(state)]
        scale = sum(jnp.sum(block * block, axis=1) for block in blocks)
        scale = lax.rsqrt(scale / width + 1e-06)
        normed = [
            (block * scale[:, None] * gain[layer][None, :]).astype(bf16)
            for block, gain in zip(blocks, gains)
        ]

        sent = jnp.concatenate(normed[:2], axis=1)
        arrived = lax.all_gather(sent, "expert", axis=0, tiled=True)
        held_a = normed[2][None]
        held_b = jnp.concatenate([normed[3], marks_sent[layer]], axis=1)[None]
        near = [columns(layer, mask, 0, units, sent) for mask in ORDER[1:3]]
        for step in range(3):
            got_a = swap(held_a, (Y_STEPS + X_STEPS)[step])
            got_b = swap(held_b, (X_STEPS + Y_STEPS)[step])
            held_a = jnp.concatenate([held_a, got_a])
            held_b = jnp.concatenate([held_b, got_b])
        held_a, held_b, *near = lax.optimization_barrier((held_a, held_b, *near))
        far = columns(layer, ORDER[3], 0, units, held_a)
        last_a, last_b = swap(held_a, X_STEPS[1]), swap(held_b, Y_STEPS[1])
        all_a = [held_a, last_a, swap(held_a, SIBLING), swap(last_a, SIBLING)]
        all_b = [held_b, last_b, swap(held_b, SIBLING), swap(last_b, SIBLING)]

        def products(tokens, mask):
            flat = [block.reshape(-1, block.shape[2]) for block in tokens]
            return first_products(z, flat, w_gate, w_up, layer, mask)

        sums_a, sums_b = products(all_a, ORDER[2]), products(all_b, ORDER[3])
        mine = lax.broadcasted_iota(jnp.int32, (1, 1, 128), 2) == me
        mark = [jnp.sum(jnp.where(mine, block[:, :, part:].astype(f32), 0.0), axis=2) for block in all_b]
        mark = jnp.dot(in_place, jnp.concatenate(mark).astype(bf16), preferred_element_type=f32)
        mark = mark.astype(jnp.int32).reshape(-1)
        arrived, sums_a, sums_b, mark, far = lax.optimization_barrier(
            (arrived, sums_a, sums_b, mark, far)
        )
        others = near + [far]
        act = gate_up(z, places, arrived, w_gate, w_up, layer, sums_a, sums_b, rows)

        source = lax.broadcasted_iota(jnp.int32, (experts, rows), 0).reshape(-1)
        slot = jnp.where(mark > 0, source * capacity + mark - 1, -1)[None, :]
        taken = (lax.broadcasted_iota(jnp.int32, (slots, 1), 0) == slot).astype(bf16)

        act = jnp.dot(taken, act, preferred_element_type=f32).astype(bf16)

        own = state.astype(f32) * scale[:, None] * norm_gain[layer][None, :]
        own = own.astype(bf16).astype(f32)
        scores = jnp.dot(own, router[layer], precision=lax.Precision.HIGHEST)
        scores = jnp.pad(jnp.concatenate(thirds(scores), axis=1), ((0, 0), (0, units - 3 * experts)))
        act = jnp.concatenate([act, scores], axis=0)
        acts = spread(act)
        scores = sum(block[slots:].astype(f32) for block in acts)
        scores = sum(scores[:, experts * n : experts * (n + 1)] for n in range(3))
        out = down_product(z, acts, slots, capacity, padded, w_down, layer, others)
        probs = jax.nn.sigmoid(scores)
        picked = jnp.where(picks[layer], probs, 0.0)
        weights = route_scale * picked / jnp.sum(picked, axis=1, keepdims=True)
        slot_iota = lax.broadcasted_iota(jnp.int32, (1, 1, padded), 2).astype(f32) + 1.0
        mixer = jnp.where(marks[layer][:, :, None] == slot_iota, weights[:, :, None], 0.0)
        mixer = jnp.concatenate(thirds(mixer.reshape(rows, experts * padded))[:2], axis=0)

        returned = lax.all_to_all(
            out.reshape(experts, padded, part), "expert", split_axis=0, concat_axis=0
        ).reshape(experts * padded, part)
        mixed = jnp.dot(mixer, returned, preferred_element_type=f32)
        state = (state.astype(f32) + mixed[:rows] + mixed[rows:]).astype(bf16)
    return state


def solution(mesh):
    placed = (
        P("expert", "tensor"),
        P(None, "tensor"),
        P(None, "tensor", None),
        P(None, "expert", None, "tensor"),
        P(None, "expert", None, "tensor"),
        P(None, "expert", "tensor", None),
        P(None, "expert", None),
    )
    return jax.shard_map(
        body, mesh=mesh, in_specs=placed, out_specs=P("expert", "tensor"), check_vma=False
    )
```

```python
import functools

import jax
import jax.numpy as jnp
from jax import lax
from jax.experimental import pallas as pl
from jax.experimental.pallas import tpu as pltpu
from jax.sharding import PartitionSpec as P

route_scale = 2.5
bf16, f32 = jnp.bfloat16, jnp.float32

SIBLING = (1, 1)
ORDER = (0, 1, 3, 2)


def short(values):
    return lax.reduce_precision(values, 8, 7)


def thirds(values):
    high = short(values)
    middle = short(values - high)
    return [part.astype(bf16) for part in (high, middle, values - high - middle)]


def swap(block, masks):
    count = lax.axis_size("expert")
    return lax.ppermute(block, "expert", [(i, i ^ masks[i & 1]) for i in range(count)])


def z_swap(block, mask):
    count = lax.axis_size("tensor")
    return lax.ppermute(block, "tensor", [(i, i ^ mask) for i in range(count)])


def after(block, *others):
    return lax.optimization_barrier((block, *others))[0]


def gate_up_kernel(layer, z_ref, tokens_ref, gate_ref, up_ref, act_ref, tokens, weights, sums, sems):
    steps, depth = weights.shape[1:3]
    copies = []
    for step, mask in enumerate(ORDER):
        features = pl.ds(pl.multiple_of((z_ref[0] ^ mask) * depth, depth), depth)
        parts = [
            (tokens_ref.at[:, pl.ds(step * depth, depth)], tokens.at[step]),
            (gate_ref.at[layer, 0, features], weights.at[0, step]),
            (up_ref.at[layer, 0, features], weights.at[1, step]),
        ]
        copies.append(
            [pltpu.make_async_copy(*part, sems.at[n, step]) for n, part in enumerate(parts)]
        )
    for copy in sum(copies, []):
        copy.start()
    for step in range(steps):
        for copy in copies[step]:
            copy.wait()
        gate = jnp.dot(tokens[step], weights[0, step], preferred_element_type=f32)
        up = jnp.dot(tokens[step], weights[1, step], preferred_element_type=f32)
        if step == 0:
            sums[0], sums[1] = gate, up
        elif step < steps - 1:
            sums[0] += gate
            sums[1] += up
        else:
            gate += sums[0]
            up += sums[1]
            act_ref[...] = (gate / (1.0 + jnp.exp(-gate)) * up).astype(act_ref.dtype)


def gate_up(z, tokens, w_gate, w_up, layer):
    rows, units = tokens.shape[0], w_gate.shape[-1]
    steps = len(ORDER)
    depth = w_gate.shape[2] // steps
    outside = pl.BlockSpec(memory_space=pl.ANY)
    return pl.pallas_call(
        functools.partial(gate_up_kernel, layer),
        in_specs=[pl.BlockSpec(memory_space=pltpu.SMEM)] + [outside] * 3,
        out_specs=pl.BlockSpec(memory_space=pltpu.VMEM),
        out_shape=jax.ShapeDtypeStruct((rows, units), bf16),
        scratch_shapes=[
            pltpu.VMEM((steps, rows, depth), bf16),
            pltpu.VMEM((2, steps, depth, units), bf16),
            pltpu.VMEM((2, rows, units), f32),
            pltpu.SemaphoreType.DMA((3, steps)),
        ],
        compiler_params=pltpu.CompilerParams(vmem_limit_bytes=58 << 20),
        cost_estimate=pl.CostEstimate(
            flops=16 * rows * depth * units,
            bytes_accessed=8 * (rows + 2 * units) * depth + 2 * rows * units,
            transcendentals=rows * units,
        ),
    )(jnp.full((1,), z, jnp.int32), tokens, w_gate, w_up)


def down_kernel(z_ref, *refs):
    acts, weights, out_ref = refs[:4], refs[4:-1], refs[-1]
    acts = jnp.concatenate([act[...] for act in acts], axis=1)
    weights = jnp.concatenate([weights[0][0, 0]] + [w[...] for w in weights[1:]], axis=0)
    out_ref[...] = jnp.dot(acts, weights, preferred_element_type=f32).astype(out_ref.dtype)


def down_product(z, acts, slots, w_down, layer, others):
    units = w_down.shape[2]
    part = others[0].shape[-1]
    steps = 2
    columns = part // steps
    act = pl.BlockSpec((slots, units), lambda n, z: (0, 0))
    return pl.pallas_call(
        down_kernel,
        grid_spec=pltpu.PrefetchScalarGridSpec(
            num_scalar_prefetch=1,
            grid=(steps,),
            in_specs=[act] * 4
            + [pl.BlockSpec((1, 1, units, columns), lambda n, z: (layer, 0, 0, z[0] * steps + n))]
            + [pl.BlockSpec((w.shape[0], columns), lambda n, z: (0, n)) for w in others],
            out_specs=pl.BlockSpec((slots, columns), lambda n, z: (0, n)),
        ),
        out_shape=jax.ShapeDtypeStruct((slots, part), bf16),
        cost_estimate=pl.CostEstimate(
            flops=8 * slots * units * part,
            bytes_accessed=8 * units * (slots + part) + 2 * slots * part,
            transcendentals=0,
        ),
    )(jnp.full((1,), z, jnp.int32), *acts, w_down, *others)


def body(hidden_in, norm_gain, router, w_gate, w_up, w_down, routes):
    rows, part = hidden_in.shape
    layers, width, units = w_gate.shape[0], w_gate.shape[2], w_gate.shape[3]
    experts = router.shape[2]
    capacity = min(rows, 2 * rows * routes.shape[2] // experts)
    slots = experts * capacity
    chips = experts // 2
    me = lax.axis_index("expert")
    core = me & 1
    z = lax.axis_index("tensor")

    expert_iota = lax.broadcasted_iota(jnp.int32, (1, 1, 1, experts), 3)
    picks = jnp.any(routes[..., None] == expert_iota, axis=2)
    earlier = lax.broadcasted_iota(jnp.int32, (rows, rows), 0) >= lax.broadcasted_iota(
        jnp.int32, (rows, rows), 1
    )
    ranks = jnp.einsum("st,lte->lse", earlier.astype(bf16), picks.astype(bf16), preferred_element_type=f32)
    marks = jnp.where(picks, ranks, 0.0)
    marks_sent = jnp.concatenate([marks[layer] for layer in range(layers)], axis=1)
    marks_sent = jnp.pad(marks_sent, ((0, 0), (0, 128 - layers * experts))).astype(bf16)

    def spread(block):
        return [block] + [z_swap(block, mask) for mask in ORDER[1:]]

    def columns(layer, mask, first, count, *bound):
        column = (after(z, *bound) ^ mask) * part
        block = lax.dynamic_slice(w_down, (layer, 0, first, column), (1, 1, count, part))
        return z_swap(block.reshape(count, part), mask)

    state = hidden_in
    gains = jnp.stack(thirds(norm_gain), axis=0).reshape(3 * layers, part)
    opening = [state, gains, jnp.zeros((8 - 3 * layers, part), bf16)]
    opening = spread(jnp.concatenate(opening, axis=0))
    gains = [
        block[rows : rows + 3 * layers].astype(f32).reshape(3, layers, part).sum(axis=0)
        for block in opening
    ]
    for layer in range(layers):
        blocks = spread(state) if layer else [block[:rows] for block in opening]
        blocks = [block.astype(f32) for block in blocks]
        scale = sum(jnp.sum(block * block, axis=1) for block in blocks)
        scale = lax.rsqrt(scale / width + 1e-06)
        normed = [
            (block * scale[:, None] * gain[layer][None, :]).astype(bf16)
            for block, gain in zip(blocks, gains)
        ]

        sent = jnp.concatenate(normed if layer else normed + [marks_sent], axis=1)
        arrived = lax.all_gather(sent, "expert", axis=0, tiled=True)
        others = [columns(layer, mask, 0, units, sent) for mask in ORDER[1:]]
        arrived, *others = lax.optimization_barrier((arrived, *others))
        if layer == 0:
            marks_here = arrived[:, width:]
        act = gate_up(z, arrived, w_gate, w_up, layer)

        mine = lax.broadcasted_iota(jnp.int32, (1, 128), 1) == me + layer * experts
        mark = jnp.sum(jnp.where(mine, marks_here.astype(f32), 0.0), axis=1).astype(jnp.int32)
        source = lax.broadcasted_iota(jnp.int32, (experts, rows), 0).reshape(-1)
        slot = jnp.where(mark > 0, source * capacity + mark - 1, -1)[None, :]
        taken = (lax.broadcasted_iota(jnp.int32, (slots, 1), 0) == slot).astype(bf16)
        act = jnp.dot(taken, act, preferred_element_type=f32).astype(bf16)

        own = state.astype(f32) * scale[:, None] * norm_gain[layer][None, :]
        own = own.astype(bf16).astype(f32)
        scores = jnp.dot(own, router[layer], precision=lax.Precision.HIGHEST)
        scores = jnp.pad(jnp.concatenate(thirds(scores), axis=1), ((0, 0), (0, units - 3 * experts)))
        act = jnp.concatenate([act, scores], axis=0)
        acts = spread(act)
        scores = sum(block[slots:].astype(f32) for block in acts)
        scores = sum(scores[:, experts * n : experts * (n + 1)] for n in range(3))
        out = down_product(z, acts, slots, w_down, layer, others)
        probs = jax.nn.sigmoid(after(scores, out))
        picked = jnp.where(picks[layer], probs, 0.0)
        weights = route_scale * picked / jnp.sum(picked, axis=1, keepdims=True)

        def mixer(parity):
            def of_parity(table):
                table = table.reshape(rows, chips, 2)
                return jnp.where(parity == 1, table[:, :, 1], table[:, :, 0])[:, :, None, None]

            shape = (1, 1, 2, capacity)
            slot = lax.broadcasted_iota(jnp.int32, shape, 3).astype(f32) + 1.0
            here = lax.broadcasted_iota(jnp.int32, shape, 2) == core
            table = jnp.where(here & (of_parity(marks[layer]) == slot), of_parity(weights), 0.0)
            return jnp.concatenate(thirds(table.reshape(rows, slots))[:2], axis=0)

        mixers = jnp.concatenate([mixer(core), swap(mixer(1 - core), SIBLING)], axis=0)
        groups = [list(range(parity, experts, 2)) for parity in range(2)]
        returned = lax.all_to_all(
            out.reshape(chips, 2 * capacity, part),
            "expert",
            split_axis=0,
            concat_axis=0,
            axis_index_groups=groups,
        ).reshape(slots, part)
        mixed = jnp.dot(mixers, returned, preferred_element_type=f32).reshape(2, 2, rows, part)
        mixed = mixed[:, 0] + mixed[:, 1]
        state = (state.astype(f32) + mixed[0] + swap(mixed[1], SIBLING)).astype(bf16)
    return state


def solution(mesh):
    placed = (
        P("expert", "tensor"),
        P(None, "tensor"),
        P(None, "tensor", None),
        P(None, "expert", None, "tensor"),
        P(None, "expert", None, "tensor"),
        P(None, "expert", "tensor", None),
        P(None, "expert", None),
    )
    return jax.shard_map(
        body, mesh=mesh, in_specs=placed, out_specs=P("expert", "tensor"), check_vma=False
    )
```

```python
import functools

import jax
import jax.numpy as jnp
from jax import lax
from jax.experimental import pallas as pl
from jax.experimental.pallas import tpu as pltpu
from jax.sharding import PartitionSpec as P

route_scale = 2.5
bf16, f32 = jnp.bfloat16, jnp.float32

SIBLING = (1, 1)
ORDER = (0, 1, 3, 2)


def short(values):
    return lax.reduce_precision(values, 8, 7)


def thirds(values):
    high = short(values)
    middle = short(values - high)
    return [part.astype(bf16) for part in (high, middle, values - high - middle)]


def swap(block, masks):
    count = lax.axis_size("expert")
    return lax.ppermute(block, "expert", [(i, i ^ masks[i & 1]) for i in range(count)])


def z_swap(block, mask):
    count = lax.axis_size("tensor")
    return lax.ppermute(block, "tensor", [(i, i ^ mask) for i in range(count)])


def after(block, *others):
    return lax.optimization_barrier((block, *others))[0]


def gate_up_kernel(
    layer, z_ref, tokens_ref, taken_ref, gate_ref, up_ref, act_ref, tokens, weights, sums, sems
):
    steps, depth = weights.shape[1:3]
    copies = []
    for step, mask in enumerate(ORDER):
        features = pl.ds(pl.multiple_of((z_ref[0] ^ mask) * depth, depth), depth)
        parts = [
            (tokens_ref.at[:, pl.ds(step * depth, depth)], tokens.at[step]),
            (gate_ref.at[layer, 0, features], weights.at[0, step]),
            (up_ref.at[layer, 0, features], weights.at[1, step]),
        ]
        copies.append(
            [pltpu.make_async_copy(*part, sems.at[n, step]) for n, part in enumerate(parts)]
        )
    for copy in sum(copies, []):
        copy.start()
    for step in range(steps):
        for copy in copies[step]:
            copy.wait()
        gate = jnp.dot(tokens[step], weights[0, step], preferred_element_type=f32)
        up = jnp.dot(tokens[step], weights[1, step], preferred_element_type=f32)
        if step == 0:
            sums[0], sums[1] = gate, up
        elif step < steps - 1:
            sums[0] += gate
            sums[1] += up
        else:
            gate += sums[0]
            up += sums[1]
            act = (gate / (1.0 + jnp.exp(-gate)) * up).astype(bf16)
            slots = jnp.dot(taken_ref[...], act, preferred_element_type=f32)
            act_ref[...] = slots.astype(act_ref.dtype)


def gate_up(z, tokens, taken, w_gate, w_up, layer):
    rows, units = tokens.shape[0], w_gate.shape[-1]
    steps = len(ORDER)
    depth = w_gate.shape[2] // steps
    outside, inside = pl.BlockSpec(memory_space=pl.ANY), pl.BlockSpec(memory_space=pltpu.VMEM)
    return pl.pallas_call(
        functools.partial(gate_up_kernel, layer),
        in_specs=[pl.BlockSpec(memory_space=pltpu.SMEM), outside, inside, outside, outside],
        out_specs=inside,
        out_shape=jax.ShapeDtypeStruct((taken.shape[0], units), bf16),
        scratch_shapes=[
            pltpu.VMEM((steps, rows, depth), bf16),
            pltpu.VMEM((2, steps, depth, units), bf16),
            pltpu.VMEM((2, rows, units), f32),
            pltpu.SemaphoreType.DMA((3, steps)),
        ],
        compiler_params=pltpu.CompilerParams(vmem_limit_bytes=56 << 20),
        cost_estimate=pl.CostEstimate(
            flops=16 * rows * depth * units,
            bytes_accessed=8 * (rows + 2 * units) * depth + 2 * rows * units,
            transcendentals=rows * units,
        ),
    )(jnp.full((1,), z, jnp.int32), tokens, taken, w_gate, w_up)


def down_kernel(layer, z_ref, a0, a1, a2, a3, down_ref, w1, w2, w3, out_ref, own, sem):
    units, part = own.shape
    column = pl.multiple_of(z_ref[0] * part, part)
    copy = pltpu.make_async_copy(down_ref.at[layer, 0, :, pl.ds(column, part)], own, sem)
    copy.start()
    acts = jnp.concatenate([a1[...], a2[...], a3[...], a0[...]], axis=1)
    copy.wait()
    half = part // 2
    for n in range(2):
        columns = slice(n * half, (n + 1) * half)
        weights = jnp.concatenate([w[:, columns] for w in (w1, w2, w3, own)], axis=0)
        out_ref[:, columns] = jnp.dot(acts, weights, preferred_element_type=f32).astype(bf16)


def down_product(z, acts, w_down, layer, others):
    slots, units = acts[0].shape
    part = others[0].shape[-1]
    outside, inside = pl.BlockSpec(memory_space=pl.ANY), pl.BlockSpec(memory_space=pltpu.VMEM)
    return pl.pallas_call(
        functools.partial(down_kernel, layer),
        in_specs=[pl.BlockSpec(memory_space=pltpu.SMEM)] + [inside] * 4 + [outside] + [inside] * 3,
        out_specs=inside,
        out_shape=jax.ShapeDtypeStruct((slots, part), bf16),
        scratch_shapes=[pltpu.VMEM((units, part), bf16), pltpu.SemaphoreType.DMA],
        compiler_params=pltpu.CompilerParams(vmem_limit_bytes=48 << 20),
        cost_estimate=pl.CostEstimate(
            flops=8 * slots * units * part,
            bytes_accessed=8 * units * (slots + part) + 2 * slots * part,
            transcendentals=0,
        ),
    )(jnp.full((1,), z, jnp.int32), *acts, w_down, *others)


def body(hidden_in, norm_gain, router, w_gate, w_up, w_down, routes):
    rows, part = hidden_in.shape
    layers, width, units = w_gate.shape[0], w_gate.shape[2], w_gate.shape[3]
    experts = router.shape[2]
    capacity = min(rows, 2 * rows * routes.shape[2] // experts)
    slots = experts * capacity
    chips = experts // 2
    me = lax.axis_index("expert")
    core = me & 1
    z = lax.axis_index("tensor")

    expert_iota = lax.broadcasted_iota(jnp.int32, (1, 1, 1, experts), 3)
    picks = jnp.any(routes[..., None] == expert_iota, axis=2)
    earlier = lax.broadcasted_iota(jnp.int32, (rows, rows), 0) >= lax.broadcasted_iota(
        jnp.int32, (rows, rows), 1
    )
    ranks = jnp.einsum("st,lte->lse", earlier.astype(bf16), picks.astype(bf16), preferred_element_type=f32)
    marks = jnp.where(picks, ranks, 0.0)
    marks_sent = jnp.concatenate([marks[layer] for layer in range(layers)], axis=1)
    marks_sent = jnp.pad(marks_sent, ((0, 0), (0, 128 - layers * experts))).astype(bf16)

    def spread(block):
        return [block] + [z_swap(block, mask) for mask in ORDER[1:]]

    def columns(layer, mask, first, count, *bound):
        column = (after(z, *bound) ^ mask) * part
        block = lax.dynamic_slice(w_down, (layer, 0, first, column), (1, 1, count, part))
        return z_swap(block.reshape(count, part), mask)

    state = hidden_in
    gains = jnp.stack(thirds(norm_gain), axis=0).reshape(3 * layers, part)
    opening = [state, gains, jnp.zeros((8 - 3 * layers, part), bf16)]
    opening = spread(jnp.concatenate(opening, axis=0))
    gains = [
        block[rows : rows + 3 * layers].astype(f32).reshape(3, layers, part).sum(axis=0)
        for block in opening
    ]
    for layer in range(layers):
        blocks = spread(state) if layer else [block[:rows] for block in opening]
        blocks = [block.astype(f32) for block in blocks]
        scale = sum(jnp.sum(block * block, axis=1) for block in blocks)
        scale = lax.rsqrt(scale / width + 1e-06)
        normed = [
            (block * scale[:, None] * gain[layer][None, :]).astype(bf16)
            for block, gain in zip(blocks, gains)
        ]

        sent = jnp.concatenate(normed if layer else normed + [marks_sent], axis=1)
        arrived = lax.all_gather(sent, "expert", axis=0, tiled=True)

        own = state.astype(f32) * scale[:, None] * norm_gain[layer][None, :]
        own = own.astype(bf16).astype(f32)
        scores = jnp.dot(own, router[layer], precision=lax.Precision.HIGHEST)
        scores = after(scores, sent)
        others = [columns(layer, mask, 0, units, scores) for mask in ORDER[1:]]
        probs = jax.nn.sigmoid(sum(spread(scores)))
        picked = jnp.where(picks[layer], probs, 0.0)
        weights = route_scale * picked / jnp.sum(picked, axis=1, keepdims=True)

        def mixer(parity):
            def of_parity(table):
                table = table.reshape(rows, chips, 2)
                return jnp.where(parity == 1, table[:, :, 1], table[:, :, 0])[:, :, None, None]

            shape = (1, 1, 2, capacity)
            slot = lax.broadcasted_iota(jnp.int32, shape, 3).astype(f32) + 1.0
            here = lax.broadcasted_iota(jnp.int32, shape, 2) == core
            table = jnp.where(here & (of_parity(marks[layer]) == slot), of_parity(weights), 0.0)
            return jnp.concatenate(thirds(table.reshape(rows, slots))[:2], axis=0)

        mixers = jnp.concatenate([mixer(core), swap(mixer(1 - core), SIBLING)], axis=0)

        def slots_of(marks_here):
            mine = lax.broadcasted_iota(jnp.int32, (1, 128), 1) == me + layer * experts
            mark = jnp.sum(jnp.where(mine, marks_here.astype(f32), 0.0), axis=1).astype(jnp.int32)
            source = lax.broadcasted_iota(jnp.int32, (experts, rows), 0).reshape(-1)
            slot = jnp.where(mark > 0, source * capacity + mark - 1, -1)[None, :]
            return (lax.broadcasted_iota(jnp.int32, (slots, 1), 0) == slot).astype(bf16)

        if layer == 0:
            arrived, mixers, *others = lax.optimization_barrier((arrived, mixers, *others))
            marks_here = arrived[:, width:]
            taken = slots_of(marks_here)
        else:
            taken = slots_of(after(marks_here, sent))
            arrived, mixers, taken, *others = lax.optimization_barrier(
                (arrived, mixers, taken, *others)
            )
        acts = spread(gate_up(z, arrived, taken, w_gate, w_up, layer))
        out = down_product(z, acts, w_down, layer, others)
        groups = [list(range(parity, experts, 2)) for parity in range(2)]
        returned = lax.all_to_all(
            out.reshape(chips, 2 * capacity, part),
            "expert",
            split_axis=0,
            concat_axis=0,
            axis_index_groups=groups,
        ).reshape(slots, part)
        mixed = jnp.dot(mixers, returned, preferred_element_type=f32).reshape(2, 2, rows, part)
        mixed = mixed[:, 0] + mixed[:, 1]
        state = (state.astype(f32) + mixed[0] + swap(mixed[1], SIBLING)).astype(bf16)
    return state


def solution(mesh):
    placed = (
        P("expert", "tensor"),
        P(None, "tensor"),
        P(None, "tensor", None),
        P(None, "expert", None, "tensor"),
        P(None, "expert", None, "tensor"),
        P(None, "expert", "tensor", None),
        P(None, "expert", None),
    )
    return jax.shard_map(
        body, mesh=mesh, in_specs=placed, out_specs=P("expert", "tensor"), check_vma=False
    )
```

```python
import functools

import jax
import jax.numpy as jnp
from jax import lax
from jax.experimental import pallas as pl
from jax.experimental.pallas import tpu as pltpu
from jax.sharding import PartitionSpec as P

route_scale = 2.5
bf16, f32 = jnp.bfloat16, jnp.float32

Y_STEPS = ((2, 6), (6, 2))
X_STEPS = ((8, 24), (24, 8))
SIBLING = (1, 1)
ORDER = (0, 1, 3, 2)


def short(values):
    return lax.reduce_precision(values, 8, 7)


def thirds(values):
    high = short(values)
    middle = short(values - high)
    return [part.astype(bf16) for part in (high, middle, values - high - middle)]


def swap(block, masks):
    count = lax.axis_size("expert")
    return lax.ppermute(block, "expert", [(i, i ^ masks[i & 1]) for i in range(count)])


def z_swap(block, mask):
    count = lax.axis_size("tensor")
    return lax.ppermute(block, "tensor", [(i, i ^ mask) for i in range(count)])


def after(block, *others):
    return lax.optimization_barrier((block, *others))[0]


def gate_up_kernel(
    layer, first, z_ref, own_ref, other_ref, gate_ref, up_ref, out_ref, tokens, weights, sems
):
    depth, units = weights.shape[2:]
    rows = own_ref.shape[0]
    copies = []
    for k in range(2):
        features = pl.ds(pl.multiple_of((z_ref[0] ^ (k ^ first)) * depth, depth), depth)
        parts = [
            (own_ref.at[:, pl.ds(k * depth, depth)], tokens.at[k, pl.ds(0, rows)]),
            (other_ref.at[:, pl.ds(k * depth, depth)], tokens.at[k, pl.ds(rows, rows)]),
            (gate_ref.at[layer, 0, features], weights.at[k, 0]),
            (up_ref.at[layer, 0, features], weights.at[k, 1]),
        ]
        copies.append(
            [pltpu.make_async_copy(*part, sems.at[k, n]) for n, part in enumerate(parts)]
        )
    for copy in sum(copies, []):
        copy.start()
    for k in range(2):
        for copy in copies[k]:
            copy.wait()
        for n in range(2):
            columns = slice(n * units, (n + 1) * units)
            product = jnp.dot(tokens[k], weights[k, n], preferred_element_type=f32)
            if k:
                product += out_ref[:, columns]
            out_ref[:, columns] = product


def gate_up(z, own, other, w_gate, w_up, layer, first):
    rows, units = own.shape[0], w_gate.shape[-1]
    depth = w_gate.shape[2] // 4
    outside, inside = pl.BlockSpec(memory_space=pl.ANY), pl.BlockSpec(memory_space=pltpu.VMEM)
    return pl.pallas_call(
        functools.partial(gate_up_kernel, layer, first),
        in_specs=[pl.BlockSpec(memory_space=pltpu.SMEM)] + [outside] * 4,
        out_specs=inside,
        out_shape=jax.ShapeDtypeStruct((2 * rows, 2 * units), f32),
        scratch_shapes=[
            pltpu.VMEM((2, 2 * rows, depth), bf16),
            pltpu.VMEM((2, 2, depth, units), bf16),
            pltpu.SemaphoreType.DMA((2, 4)),
        ],
        compiler_params=pltpu.CompilerParams(vmem_limit_bytes=58 << 20),
        cost_estimate=pl.CostEstimate(
            flops=16 * rows * depth * units,
            bytes_accessed=8 * (rows + units) * depth + 16 * rows * units,
            transcendentals=0,
        ),
    )(jnp.full((1,), z, jnp.int32), own, other, w_gate, w_up)


def down_kernel(layer, slots, z_ref, a0, a1, a2, a3, down_ref, *refs):
    others, (out_ref, weights, sems) = refs[:-3], refs[-3:]
    units, part = down_ref.shape[2], out_ref.shape[1]
    column = pl.multiple_of(z_ref[0] * part, part)
    sources = [down_ref.at[layer, 0, :, pl.ds(column, part)]] + list(others)
    copies, row = [], 0
    for n, source in enumerate(sources):
        target = weights.at[pl.ds(row, source.shape[0])]
        copies.append(pltpu.make_async_copy(source, target, sems.at[n]))
        row += source.shape[0]
    for copy in copies:
        copy.start()
    acts = jnp.concatenate([a[:slots] for a in (a0, a1, a2, a3)], axis=1)
    for copy in copies:
        copy.wait()
    half = part // 2
    for n in range(2):
        columns = slice(n * half, (n + 1) * half)
        product = jnp.dot(acts, weights[:, columns], preferred_element_type=f32)
        out_ref[:, columns] = product.astype(bf16)


def down_product(z, acts, slots, w_down, layer, others):
    units, part = w_down.shape[2], others[0].shape[-1]
    outside, inside = pl.BlockSpec(memory_space=pl.ANY), pl.BlockSpec(memory_space=pltpu.VMEM)
    return pl.pallas_call(
        functools.partial(down_kernel, layer, slots),
        in_specs=[pl.BlockSpec(memory_space=pltpu.SMEM)]
        + [inside] * 4
        + [outside] * (1 + len(others)),
        out_specs=inside,
        out_shape=jax.ShapeDtypeStruct((slots, part), bf16),
        scratch_shapes=[
            pltpu.VMEM((4 * units, part), bf16),
            pltpu.SemaphoreType.DMA((1 + len(others),)),
        ],
        compiler_params=pltpu.CompilerParams(vmem_limit_bytes=48 << 20),
        cost_estimate=pl.CostEstimate(
            flops=8 * slots * units * part,
            bytes_accessed=8 * units * (slots + part) + 2 * slots * part,
            transcendentals=0,
        ),
    )(jnp.full((1,), z, jnp.int32), *acts, w_down, *others)


def body(hidden_in, norm_gain, router, w_gate, w_up, w_down, routes):
    rows, part = hidden_in.shape
    layers, width, units = w_gate.shape[0], w_gate.shape[2], w_gate.shape[3]
    experts = router.shape[2]
    capacity = min(rows, 2 * rows * routes.shape[2] // experts)
    slots = experts * capacity
    chips = experts // 2
    me = lax.axis_index("expert")
    core = me & 1
    z = lax.axis_index("tensor")

    bits = jnp.arange(chips, dtype=jnp.int32)
    sources = []
    for c in range(2):
        masks = [Y_STEPS[0][c], Y_STEPS[1][c], X_STEPS[0][c], X_STEPS[1][c]]
        total = jnp.zeros_like(bits)
        for n, mask in enumerate(masks):
            total = total ^ jnp.where(((bits >> n) & 1) == 1, mask, 0)
        sources.append(total)
    own_source = me ^ jnp.where(core == 1, sources[1], sources[0])
    other_source = (me ^ 1) ^ jnp.where(core == 1, sources[0], sources[1])
    source = jnp.concatenate([own_source, other_source])

    expert_iota = lax.broadcasted_iota(jnp.int32, (1, 1, 1, experts), 3)
    picks = jnp.any(routes[..., None] == expert_iota, axis=2)
    earlier = lax.broadcasted_iota(jnp.int32, (rows, rows), 0) >= lax.broadcasted_iota(
        jnp.int32, (rows, rows), 1
    )
    ranks = jnp.einsum("st,lte->lse", earlier.astype(bf16), picks.astype(bf16), preferred_element_type=f32)
    marks = jnp.where(picks, ranks, 0.0)
    marks_sent = jnp.concatenate([marks[layer] for layer in range(layers)], axis=1)
    marks_sent = jnp.pad(marks_sent, ((0, 0), (0, 128 - layers * experts))).astype(bf16)

    def spread(block):
        return [block] + [z_swap(block, mask) for mask in ORDER[1:]]

    def columns(layer, mask, first, count, *bound):
        column = (after(z, *bound) ^ mask) * part
        block = lax.dynamic_slice(w_down, (layer, 0, first, column), (1, 1, count, part))
        return block.reshape(count, part)

    def reshard(layer, mask, first, count, *bound):
        return z_swap(columns(layer, mask, first, count, *bound), mask)

    state = hidden_in
    gains = jnp.stack(thirds(norm_gain), axis=0).reshape(3 * layers, part)
    opening = [state, gains, jnp.zeros((8 - 3 * layers, part), bf16)]
    opening = spread(jnp.concatenate(opening, axis=0))
    gains = [
        block[rows : rows + 3 * layers].astype(f32).reshape(3, layers, part).sum(axis=0)
        for block in opening
    ]
    for layer in range(layers):
        blocks = spread(state) if layer else [block[:rows] for block in opening]
        blocks = [block.astype(f32) for block in blocks]
        scale = sum(jnp.sum(block * block, axis=1) for block in blocks)
        scale = lax.rsqrt(scale / width + 1e-06)
        normed = [
            (block * scale[:, None] * gain[layer][None, :]).astype(bf16)
            for block, gain in zip(blocks, gains)
        ]

        held_a = jnp.concatenate(normed[:2], axis=1)[None]
        held_b = jnp.concatenate(normed[2:] + [marks_sent] * (layer == 0), axis=1)[None]
        part_units = units // 2
        if layer == 0:
            near = [reshard(layer, mask, 0, part_units, held_a) for mask in ORDER[1:3]]
        far = [columns(layer, ORDER[3], 0, part_units, held_a)]
        far += [columns(layer, ORDER[3], part_units, part_units, held_a)]
        for step in range(3):
            if step == 2:
                held_a, held_b, far[0], *near = lax.optimization_barrier(
                    (held_a, held_b, far[0], *near)
                )
                if layer == 0:
                    more = [
                        reshard(layer, mask, part_units, part_units, held_a, held_b)
                        for mask in ORDER[1:3]
                    ]
                else:
                    far[0] = z_swap(far[0], ORDER[3])
            got_a = swap(held_a, (Y_STEPS + X_STEPS)[step])
            got_b = swap(held_b, (X_STEPS + Y_STEPS)[step])
            held_a = jnp.concatenate([held_a, got_a])
            held_b = jnp.concatenate([held_b, got_b])
        if layer == 0:
            held_a, held_b, *rest = lax.optimization_barrier((held_a, held_b, *far, *more))
            far, more = rest[:2], rest[2:]
            far[0] = z_swap(far[0], ORDER[3])
            near = [near[0], more[0], near[1], more[1]]
        else:
            held_a, held_b, *far = lax.optimization_barrier((held_a, held_b, *far))
        far[1] = z_swap(far[1], ORDER[3])
        last_a, last_b = swap(held_a, X_STEPS[1]), swap(held_b, Y_STEPS[1])
        other_a, other_b = swap(held_a, SIBLING), swap(held_b, SIBLING)

        def products(own, other, first):
            flat = [block.reshape(-1, block.shape[2]) for block in (own, other)]
            return gate_up(z, *flat, w_gate, w_up, layer, first)

        sums_a = products(held_a, other_a, 0)
        sums_b = products(held_b, other_b, 3)
        last_a, last_b, sums_a, sums_b, *far = lax.optimization_barrier(
            (last_a, last_b, sums_a, sums_b, *far)
        )
        last_other_a, last_other_b = swap(last_a, SIBLING), swap(last_b, SIBLING)
        more_a = products(last_a, last_other_a, 0)
        more_b = products(last_b, last_other_b, 3)

        if layer == 0:
            mark_blocks = [block[:, :, width // 2 :] for block in (held_b, last_b, other_b, last_other_b)]
        mine = lax.broadcasted_iota(jnp.int32, (1, 1, 128), 2) == me + layer * experts
        mark = [
            jnp.sum(jnp.where(mine, block.astype(f32), 0.0), axis=2) for block in mark_blocks
        ]
        mark = jnp.concatenate(mark).reshape(2, 4, 4, rows).swapaxes(1, 2).reshape(2 * chips, rows)
        mark = mark.astype(jnp.int32)
        slot = jnp.where(mark > 0, source[:, None] * capacity + mark - 1, -1).reshape(1, -1)
        taken = (lax.broadcasted_iota(jnp.int32, (slots, 1), 0) == slot).astype(bf16)

        def in_order(held, last):
            blocks = (2, 2, 4, rows, 2 * units)
            return jnp.concatenate([held.reshape(blocks), last.reshape(blocks)], axis=1)

        sums = in_order(sums_a, more_a) + in_order(sums_b, more_b).swapaxes(1, 2)
        sums = sums.reshape(2 * chips * rows, 2 * units)
        act = (jax.nn.silu(sums[:, :units]) * sums[:, units:]).astype(bf16)
        act = jnp.dot(taken, act, preferred_element_type=f32).astype(bf16)

        own = state.astype(f32) * scale[:, None] * norm_gain[layer][None, :]
        own = own.astype(bf16).astype(f32)
        scores = jnp.dot(own, router[layer], precision=lax.Precision.HIGHEST)
        scores = jnp.pad(jnp.concatenate(thirds(scores), axis=1), ((0, 0), (0, units - 3 * experts)))
        acts = spread(jnp.concatenate([act, scores], axis=0))
        out = down_product(z, acts, slots, w_down, layer, near + far)
        scores = sum(block[slots:].astype(f32) for block in acts)
        scores = sum(scores[:, experts * n : experts * (n + 1)] for n in range(3))
        probs = jax.nn.sigmoid(after(scores, out))
        picked = jnp.where(picks[layer], probs, 0.0)
        weights = route_scale * picked / jnp.sum(picked, axis=1, keepdims=True)

        def mixer(parity):
            def of_parity(table):
                table = table.reshape(rows, chips, 2)
                return jnp.where(parity == 1, table[:, :, 1], table[:, :, 0])[:, :, None, None]

            shape = (1, 1, 2, capacity)
            slot = lax.broadcasted_iota(jnp.int32, shape, 3).astype(f32) + 1.0
            here = lax.broadcasted_iota(jnp.int32, shape, 2) == core
            table = jnp.where(here & (of_parity(marks[layer]) == slot), of_parity(weights), 0.0)
            return jnp.concatenate(thirds(table.reshape(rows, slots))[:2], axis=0)

        mixers = jnp.concatenate([mixer(core), swap(mixer(1 - core), SIBLING)], axis=0)
        groups = [list(range(parity, experts, 2)) for parity in range(2)]
        returned = lax.all_to_all(
            out.reshape(chips, 2 * capacity, part),
            "expert",
            split_axis=0,
            concat_axis=0,
            axis_index_groups=groups,
        ).reshape(slots, part)
        if layer + 1 < layers:
            near = [reshard(layer + 1, mask, 0, units, out) for mask in ORDER[1:3]]
            returned, *near = lax.optimization_barrier((returned, *near))
        mixed = jnp.dot(mixers, returned, preferred_element_type=f32).reshape(2, 2, rows, part)
        mixed = mixed[:, 0] + mixed[:, 1]
        state = (state.astype(f32) + mixed[0] + swap(mixed[1], SIBLING)).astype(bf16)
    return state


def solution(mesh):
    placed = (
        P("expert", "tensor"),
        P(None, "tensor"),
        P(None, "tensor", None),
        P(None, "expert", None, "tensor"),
        P(None, "expert", None, "tensor"),
        P(None, "expert", "tensor", None),
        P(None, "expert", None),
    )
    return jax.shard_map(
        body, mesh=mesh, in_specs=placed, out_specs=P("expert", "tensor"), check_vma=False
    )
```

```python
import functools

import jax
import jax.numpy as jnp
from jax import lax
from jax.experimental import pallas as pl
from jax.experimental.pallas import tpu as pltpu
from jax.sharding import PartitionSpec as P

route_scale = 2.5
bf16, f32 = jnp.bfloat16, jnp.float32

Y_STEPS = ((2, 6), (6, 2))
X_STEPS = ((8, 24), (24, 8))
SIBLING = (1, 1)
ORDER = (0, 1, 3, 2)


def short(values):
    return lax.reduce_precision(values, 8, 7)


def thirds(values):
    high = short(values)
    middle = short(values - high)
    return [part.astype(bf16) for part in (high, middle, values - high - middle)]


def swap(block, masks):
    count = lax.axis_size("expert")
    return lax.ppermute(block, "expert", [(i, i ^ masks[i & 1]) for i in range(count)])


def z_swap(block, mask):
    count = lax.axis_size("tensor")
    return lax.ppermute(block, "tensor", [(i, i ^ mask) for i in range(count)])


def after(block, *others):
    return lax.optimization_barrier((block, *others))[0]


def gate_up_kernel(
    layer, z_ref, tokens_ref, taken_ref, gate_ref, up_ref, act_ref, tokens, weights, sums, sems
):
    steps, depth = weights.shape[1:3]
    copies = []
    for step, mask in enumerate(ORDER):
        features = pl.ds(pl.multiple_of((z_ref[0] ^ mask) * depth, depth), depth)
        parts = [
            (tokens_ref.at[:, pl.ds(step * depth, depth)], tokens.at[step]),
            (gate_ref.at[layer, 0, features], weights.at[0, step]),
            (up_ref.at[layer, 0, features], weights.at[1, step]),
        ]
        copies.append(
            [pltpu.make_async_copy(*part, sems.at[n, step]) for n, part in enumerate(parts)]
        )
    for copy in sum(copies, []):
        copy.start()
    for step in range(steps):
        for copy in copies[step]:
            copy.wait()
        gate = jnp.dot(tokens[step], weights[0, step], preferred_element_type=f32)
        up = jnp.dot(tokens[step], weights[1, step], preferred_element_type=f32)
        if step == 0:
            sums[0], sums[1] = gate, up
        elif step < steps - 1:
            sums[0] += gate
            sums[1] += up
        else:
            gate += sums[0]
            up += sums[1]
            act = (gate / (1.0 + jnp.exp(-gate)) * up).astype(bf16)
            slots = jnp.dot(taken_ref[...], act, preferred_element_type=f32)
            act_ref[...] = slots.astype(act_ref.dtype)


def gate_up(z, tokens, taken, w_gate, w_up, layer):
    rows, units = tokens.shape[0], w_gate.shape[-1]
    steps = len(ORDER)
    depth = w_gate.shape[2] // steps
    outside, inside = pl.BlockSpec(memory_space=pl.ANY), pl.BlockSpec(memory_space=pltpu.VMEM)
    return pl.pallas_call(
        functools.partial(gate_up_kernel, layer),
        in_specs=[pl.BlockSpec(memory_space=pltpu.SMEM), outside, inside, outside, outside],
        out_specs=inside,
        out_shape=jax.ShapeDtypeStruct((taken.shape[0], units), bf16),
        scratch_shapes=[
            pltpu.VMEM((steps, rows, depth), bf16),
            pltpu.VMEM((2, steps, depth, units), bf16),
            pltpu.VMEM((2, rows, units), f32),
            pltpu.SemaphoreType.DMA((3, steps)),
        ],
        compiler_params=pltpu.CompilerParams(vmem_limit_bytes=56 << 20),
        cost_estimate=pl.CostEstimate(
            flops=16 * rows * depth * units,
            bytes_accessed=8 * (rows + 2 * units) * depth + 2 * rows * units,
            transcendentals=rows * units,
        ),
    )(jnp.full((1,), z, jnp.int32), tokens, taken, w_gate, w_up)


def down_kernel(layer, z_ref, a0, a1, a2, a3, down_ref, w1, w2, w3, out_ref, own, act, sems):
    units, part = own.shape
    column = pl.multiple_of(z_ref[0] * part, part)
    copies = [
        pltpu.make_async_copy(down_ref.at[layer, 0, :, pl.ds(column, part)], own, sems.at[0]),
        pltpu.make_async_copy(a0, act, sems.at[1]),
    ]
    for copy in copies:
        copy.start()
    for copy in copies:
        copy.wait()
    acts = jnp.concatenate([a1[...], a2[...], a3[...], act[...]], axis=1)
    half = part // 2
    for n in range(2):
        columns = slice(n * half, (n + 1) * half)
        weights = jnp.concatenate([w[:, columns] for w in (w1, w2, w3, own)], axis=0)
        out_ref[:, columns] = jnp.dot(acts, weights, preferred_element_type=f32).astype(bf16)


def down_product(z, acts, w_down, layer, others):
    slots, units = acts[0].shape
    part = others[0].shape[-1]
    outside, inside = pl.BlockSpec(memory_space=pl.ANY), pl.BlockSpec(memory_space=pltpu.VMEM)
    return pl.pallas_call(
        functools.partial(down_kernel, layer),
        in_specs=[pl.BlockSpec(memory_space=pltpu.SMEM), outside]
        + [inside] * 3
        + [outside]
        + [inside] * 3,
        out_specs=inside,
        out_shape=jax.ShapeDtypeStruct((slots, part), bf16),
        scratch_shapes=[
            pltpu.VMEM((units, part), bf16),
            pltpu.VMEM((slots, units), bf16),
            pltpu.SemaphoreType.DMA((2,)),
        ],
        compiler_params=pltpu.CompilerParams(vmem_limit_bytes=48 << 20),
        cost_estimate=pl.CostEstimate(
            flops=8 * slots * units * part,
            bytes_accessed=8 * units * (slots + part) + 2 * slots * part,
            transcendentals=0,
        ),
    )(jnp.full((1,), z, jnp.int32), *acts, w_down, *others)


def body(hidden_in, norm_gain, router, w_gate, w_up, w_down, routes):
    rows, part = hidden_in.shape
    layers, width, units = w_gate.shape[0], w_gate.shape[2], w_gate.shape[3]
    experts = router.shape[2]
    capacity = min(rows, 2 * rows * routes.shape[2] // experts)
    slots = experts * capacity
    chips = experts // 2
    quarters = lax.axis_size("tensor")
    me = lax.axis_index("expert")
    core = me & 1
    z = lax.axis_index("tensor")

    away = lax.broadcasted_iota(jnp.int32, (experts,), 0) ^ me
    odd = ((away ^ me) & 1) == 1

    def turns(distance):
        low, high = (distance & 1) ^ (distance >> 1), distance >> 1
        return jnp.where(odd, high, low) + 2 * jnp.where(odd, low, high)

    places = (away & 1) * chips + turns((away >> 1) & 3) + 4 * turns(away >> 3)
    in_place = places[:, None] == lax.broadcasted_iota(jnp.int32, (1, experts), 1)

    expert_iota = lax.broadcasted_iota(jnp.int32, (1, 1, 1, experts), 3)
    picks = jnp.any(routes[..., None] == expert_iota, axis=2)
    earlier = lax.broadcasted_iota(jnp.int32, (rows, rows), 0) >= lax.broadcasted_iota(
        jnp.int32, (rows, rows), 1
    )
    ranks = jnp.einsum("st,lte->lse", earlier.astype(bf16), picks.astype(bf16), preferred_element_type=f32)
    marks = jnp.where(picks, ranks, 0.0)
    marks_sent = jnp.concatenate([marks[layer] for layer in range(layers)], axis=1)
    marks_sent = jnp.pad(marks_sent, ((0, 0), (0, 128 - layers * experts))).astype(bf16)

    def spread(block):
        return [block] + [z_swap(block, mask) for mask in ORDER[1:]]

    def columns(layer, mask, first, count, *bound):
        column = (after(z, *bound) ^ mask) * part
        block = lax.dynamic_slice(w_down, (layer, 0, first, column), (1, 1, count, part))
        return z_swap(block.reshape(count, part), mask)

    def slots_of(marks_here, layer):
        mine = lax.broadcasted_iota(jnp.int32, (1, 1, 128), 2) == me + layer * experts
        mark = jnp.sum(jnp.where(mine, marks_here, 0.0), axis=2).astype(bf16)
        mark = jnp.dot(in_place.astype(bf16), mark, preferred_element_type=f32).astype(jnp.int32)
        source = lax.broadcasted_iota(jnp.int32, (experts, 1), 0)
        slot = jnp.where(mark > 0, source * capacity + mark - 1, -1).reshape(1, -1)
        return (lax.broadcasted_iota(jnp.int32, (slots, 1), 0) == slot).astype(bf16)

    state = hidden_in
    gains = jnp.stack(thirds(norm_gain), axis=0).reshape(3 * layers, part)
    opening = [state, gains, jnp.zeros((8 - 3 * layers, part), bf16)]
    opening = spread(jnp.concatenate(opening, axis=0))
    gains = [
        block[rows : rows + 3 * layers].astype(f32).reshape(3, layers, part).sum(axis=0)
        for block in opening
    ]
    for layer in range(layers):
        blocks = spread(state) if layer else [block[:rows] for block in opening]
        blocks = [block.astype(f32) for block in blocks]
        scale = sum(jnp.sum(block * block, axis=1) for block in blocks)
        scale = lax.rsqrt(scale / width + 1e-06)
        normed = [
            (block * scale[:, None] * gain[layer][None, :]).astype(bf16)
            for block, gain in zip(blocks, gains)
        ]

        sent = jnp.concatenate(normed, axis=1)
        arrived = lax.all_gather(sent, "expert", axis=0, tiled=True)

        own = state.astype(f32) * scale[:, None] * norm_gain[layer][None, :]
        own = own.astype(bf16).astype(f32)
        scores = jnp.dot(own, router[layer], precision=lax.Precision.HIGHEST)
        scores = after(scores, sent)
        others = [columns(layer, mask, 0, units, scores) for mask in ORDER[1:]]
        probs = jax.nn.sigmoid(sum(spread(scores)))
        picked = jnp.where(picks[layer], probs, 0.0)
        weights = route_scale * picked / jnp.sum(picked, axis=1, keepdims=True)

        def mixer(parity):
            def of_parity(table):
                table = table.reshape(rows, chips, 2)
                return jnp.where(parity == 1, table[:, :, 1], table[:, :, 0])[:, :, None, None]

            shape = (1, 1, 2, capacity)
            slot = lax.broadcasted_iota(jnp.int32, shape, 3).astype(f32) + 1.0
            here = lax.broadcasted_iota(jnp.int32, shape, 2) == core
            table = jnp.where(here & (of_parity(marks[layer]) == slot), of_parity(weights), 0.0)
            return jnp.concatenate(thirds(table.reshape(rows, slots))[:2], axis=0)

        mixers = jnp.concatenate([mixer(core), swap(mixer(1 - core), SIBLING)], axis=0)

        if layer == 0:
            held = after(marks_sent, scores)[None]
            for masks in Y_STEPS + X_STEPS:
                held = jnp.concatenate([held, swap(held, masks)])
            held = jnp.concatenate([held, swap(held, SIBLING)]).astype(f32)
            taken = [slots_of(held, each) for each in range(layers)]
            arrived, mixers, taken, others = lax.optimization_barrier(
                (arrived, mixers, taken, others)
            )
        else:
            arrived, mixers, others = lax.optimization_barrier((arrived, mixers, others))
        acts = spread(gate_up(z, arrived, taken[layer], w_gate, w_up, layer))
        acts[0] = jnp.where(z < quarters, acts[0], 0.0)
        out = down_product(z, acts, w_down, layer, others)
        groups = [list(range(parity, experts, 2)) for parity in range(2)]
        returned = lax.all_to_all(
            out.reshape(chips, 2 * capacity, part),
            "expert",
            split_axis=0,
            concat_axis=0,
            axis_index_groups=groups,
        ).reshape(slots, part)
        mixed = jnp.dot(mixers, returned, preferred_element_type=f32).reshape(2, 2, rows, part)
        mixed = mixed[:, 0] + mixed[:, 1]
        state = (state.astype(f32) + mixed[0] + swap(mixed[1], SIBLING)).astype(bf16)
    return state


def solution(mesh):
    placed = (
        P("expert", "tensor"),
        P(None, "tensor"),
        P(None, "tensor", None),
        P(None, "expert", None, "tensor"),
        P(None, "expert", None, "tensor"),
        P(None, "expert", "tensor", None),
        P(None, "expert", None),
    )
    return jax.shard_map(
        body, mesh=mesh, in_specs=placed, out_specs=P("expert", "tensor"), check_vma=False
    )
```

```python
import functools

import jax
import jax.numpy as jnp
from jax import lax
from jax.experimental import pallas as pl
from jax.experimental.pallas import tpu as pltpu
from jax.sharding import PartitionSpec as P

route_scale = 2.5
bf16, f32 = jnp.bfloat16, jnp.float32

Y_STEPS = ((2, 6), (6, 2))
X_STEPS = ((8, 24), (24, 8))
SIBLING = (1, 1)
ORDER = (0, 1, 3, 2)


def short(values):
    return lax.reduce_precision(values, 8, 7)


def thirds(values):
    high = short(values)
    middle = short(values - high)
    return [part.astype(bf16) for part in (high, middle, values - high - middle)]


def swap(block, masks):
    count = lax.axis_size("expert")
    return lax.ppermute(block, "expert", [(i, i ^ masks[i & 1]) for i in range(count)])


def z_swap(block, mask):
    count = lax.axis_size("tensor")
    return lax.ppermute(block, "tensor", [(i, i ^ mask) for i in range(count)])


def after(block, *others):
    return lax.optimization_barrier((block, *others))[0]


def gate_up_kernel(
    layer, z_ref, tokens_ref, taken_ref, gate_ref, up_ref, act_ref, tokens, weights, sums, sems
):
    steps, depth = weights.shape[1:3]
    copies = []
    for step, mask in enumerate(ORDER):
        features = pl.ds(pl.multiple_of((z_ref[0] ^ mask) * depth, depth), depth)
        parts = [
            (tokens_ref.at[:, pl.ds(step * depth, depth)], tokens.at[step]),
            (gate_ref.at[layer, 0, features], weights.at[0, step]),
            (up_ref.at[layer, 0, features], weights.at[1, step]),
        ]
        copies.append(
            [pltpu.make_async_copy(*part, sems.at[n, step]) for n, part in enumerate(parts)]
        )
    for copy in sum(copies, []):
        copy.start()
    for step in range(steps):
        for copy in copies[step]:
            copy.wait()
        gate = jnp.dot(tokens[step], weights[0, step], preferred_element_type=f32)
        up = jnp.dot(tokens[step], weights[1, step], preferred_element_type=f32)
        if step == 0:
            sums[0], sums[1] = gate, up
        elif step < steps - 1:
            sums[0] += gate
            sums[1] += up
        else:
            gate += sums[0]
            up += sums[1]
            act = (gate / (1.0 + jnp.exp(-gate)) * up).astype(bf16)
            slots = jnp.dot(taken_ref[...], act, preferred_element_type=f32)
            act_ref[...] = slots.astype(act_ref.dtype)


def gate_up(z, tokens, taken, w_gate, w_up, layer):
    rows, units = tokens.shape[0], w_gate.shape[-1]
    steps = len(ORDER)
    depth = w_gate.shape[2] // steps
    outside, inside = pl.BlockSpec(memory_space=pl.ANY), pl.BlockSpec(memory_space=pltpu.VMEM)
    return pl.pallas_call(
        functools.partial(gate_up_kernel, layer),
        in_specs=[pl.BlockSpec(memory_space=pltpu.SMEM), outside, inside, outside, outside],
        out_specs=inside,
        out_shape=jax.ShapeDtypeStruct((taken.shape[0], units), bf16),
        scratch_shapes=[
            pltpu.VMEM((steps, rows, depth), bf16),
            pltpu.VMEM((2, steps, depth, units), bf16),
            pltpu.VMEM((2, rows, units), f32),
            pltpu.SemaphoreType.DMA((3, steps)),
        ],
        compiler_params=pltpu.CompilerParams(vmem_limit_bytes=56 << 20),
        cost_estimate=pl.CostEstimate(
            flops=16 * rows * depth * units,
            bytes_accessed=8 * (rows + 2 * units) * depth + 2 * rows * units,
            transcendentals=rows * units,
        ),
    )(jnp.full((1,), z, jnp.int32), tokens, taken, w_gate, w_up)


def down_kernel(layer, z_ref, a0, a1, a2, a3, down_ref, w1, w2, w3, out_ref, own, act, sems):
    units, part = own.shape
    column = pl.multiple_of(z_ref[0] * part, part)
    copies = [
        pltpu.make_async_copy(down_ref.at[layer, 0, :, pl.ds(column, part)], own, sems.at[0]),
        pltpu.make_async_copy(a0, act, sems.at[1]),
    ]
    for copy in copies:
        copy.start()
    for copy in copies:
        copy.wait()
    acts = jnp.concatenate([a1[...], a2[...], a3[...], act[...]], axis=1)
    half = part // 2
    for n in range(2):
        columns = slice(n * half, (n + 1) * half)
        weights = jnp.concatenate([w[:, columns] for w in (w1, w2, w3, own)], axis=0)
        out_ref[:, columns] = jnp.dot(acts, weights, preferred_element_type=f32).astype(bf16)


def down_product(z, acts, w_down, layer, others):
    slots, units = acts[0].shape
    part = others[0].shape[-1]
    outside, inside = pl.BlockSpec(memory_space=pl.ANY), pl.BlockSpec(memory_space=pltpu.VMEM)
    return pl.pallas_call(
        functools.partial(down_kernel, layer),
        in_specs=[pl.BlockSpec(memory_space=pltpu.SMEM), outside]
        + [inside] * 3
        + [outside]
        + [inside] * 3,
        out_specs=inside,
        out_shape=jax.ShapeDtypeStruct((slots, part), bf16),
        scratch_shapes=[
            pltpu.VMEM((units, part), bf16),
            pltpu.VMEM((slots, units), bf16),
            pltpu.SemaphoreType.DMA((2,)),
        ],
        compiler_params=pltpu.CompilerParams(vmem_limit_bytes=48 << 20),
        cost_estimate=pl.CostEstimate(
            flops=8 * slots * units * part,
            bytes_accessed=8 * units * (slots + part) + 2 * slots * part,
            transcendentals=0,
        ),
    )(jnp.full((1,), z, jnp.int32), *acts, w_down, *others)


def body(hidden_in, norm_gain, router, w_gate, w_up, w_down, routes):
    rows, part = hidden_in.shape
    layers, width, units = w_gate.shape[0], w_gate.shape[2], w_gate.shape[3]
    experts = router.shape[2]
    capacity = min(rows, 2 * rows * routes.shape[2] // experts)
    slots = experts * capacity
    chips = experts // 2
    quarters = lax.axis_size("tensor")
    me = lax.axis_index("expert")
    core = me & 1
    z = lax.axis_index("tensor")

    away = lax.broadcasted_iota(jnp.int32, (experts,), 0) ^ me
    odd = ((away ^ me) & 1) == 1

    def turns(distance):
        low, high = (distance & 1) ^ (distance >> 1), distance >> 1
        return jnp.where(odd, high, low) + 2 * jnp.where(odd, low, high)

    places = (away & 1) * chips + turns((away >> 1) & 3) + 4 * turns(away >> 3)
    in_place = places[:, None] == lax.broadcasted_iota(jnp.int32, (1, experts), 1)

    expert_iota = lax.broadcasted_iota(jnp.int32, (1, 1, 1, experts), 3)
    picks = jnp.any(routes[..., None] == expert_iota, axis=2)
    earlier = lax.broadcasted_iota(jnp.int32, (rows, rows), 0) >= lax.broadcasted_iota(
        jnp.int32, (rows, rows), 1
    )
    ranks = jnp.einsum("st,lte->lse", earlier.astype(bf16), picks.astype(bf16), preferred_element_type=f32)
    marks = jnp.where(picks, ranks, 0.0)
    marks_sent = jnp.concatenate([marks[layer] for layer in range(layers)], axis=1)
    marks_sent = jnp.pad(marks_sent, ((0, 0), (0, 128 - layers * experts))).astype(bf16)

    def spread(block):
        return [block] + [z_swap(block, mask) for mask in ORDER[1:]]

    def columns(layer, mask, first, count, *bound):
        column = (after(z, *bound) ^ mask) * part
        block = lax.dynamic_slice(w_down, (layer, 0, first, column), (1, 1, count, part))
        return z_swap(block.reshape(count, part), mask)

    def slots_of(marks_here, layer):
        mine = lax.broadcasted_iota(jnp.int32, (1, 1, 128), 2) == me + layer * experts
        mark = jnp.sum(jnp.where(mine, marks_here, 0.0), axis=2).astype(bf16)
        mark = jnp.dot(in_place.astype(bf16), mark, preferred_element_type=f32).astype(jnp.int32)
        source = lax.broadcasted_iota(jnp.int32, (experts, 1), 0)
        slot = jnp.where(mark > 0, source * capacity + mark - 1, -1).reshape(1, -1)
        return (lax.broadcasted_iota(jnp.int32, (slots, 1), 0) == slot).astype(bf16)

    state = hidden_in
    opening = [state, norm_gain.astype(bf16), jnp.zeros((8 - layers, part), bf16)]
    opening = spread(jnp.concatenate(opening, axis=0))
    gains = [block[rows : rows + layers].astype(f32) for block in opening]
    for layer in range(layers):
        blocks = spread(state) if layer else [block[:rows] for block in opening]
        blocks = [block.astype(f32) for block in blocks]
        scale = sum(jnp.sum(block * block, axis=1) for block in blocks)
        scale = lax.rsqrt(scale / width + 1e-06)
        normed = [
            (block * scale[:, None] * gain[layer][None, :]).astype(bf16)
            for block, gain in zip(blocks, gains)
        ]

        sent = jnp.concatenate(normed, axis=1)
        arrived = lax.all_gather(sent, "expert", axis=0, tiled=True)

        own = state.astype(f32) * scale[:, None] * norm_gain[layer][None, :]
        own = own.astype(bf16).astype(f32)
        scores = jnp.dot(own, router[layer], precision=lax.Precision.HIGHEST)
        scores = after(scores, sent)
        others = [columns(layer, mask, 0, units, scores) for mask in ORDER[1:]]
        probs = jax.nn.sigmoid(sum(spread(scores)))
        picked = jnp.where(picks[layer], probs, 0.0)
        weights = route_scale * picked / jnp.sum(picked, axis=1, keepdims=True)

        def mixer(parity):
            def of_parity(table):
                table = table.reshape(rows, chips, 2)
                return jnp.where(parity == 1, table[:, :, 1], table[:, :, 0])[:, :, None, None]

            shape = (1, 1, 2, capacity)
            slot = lax.broadcasted_iota(jnp.int32, shape, 3).astype(f32) + 1.0
            here = lax.broadcasted_iota(jnp.int32, shape, 2) == core
            table = jnp.where(here & (of_parity(marks[layer]) == slot), of_parity(weights), 0.0)
            return jnp.concatenate(thirds(table.reshape(rows, slots))[:2], axis=0)

        mixers = jnp.concatenate([mixer(core), swap(mixer(1 - core), SIBLING)], axis=0)

        if layer == 0:
            held = after(marks_sent, scores)[None]
            for masks in Y_STEPS + X_STEPS:
                held = jnp.concatenate([held, swap(held, masks)])
            held = jnp.concatenate([held, swap(held, SIBLING)]).astype(f32)
            taken = [slots_of(held, each) for each in range(layers)]
            arrived, mixers, taken, others = lax.optimization_barrier(
                (arrived, mixers, taken, others)
            )
        else:
            arrived, mixers, others = lax.optimization_barrier((arrived, mixers, others))
        acts = spread(gate_up(z, arrived, taken[layer], w_gate, w_up, layer))
        acts[0] = jnp.where(z < quarters, acts[0], 0.0)
        out = down_product(z, acts, w_down, layer, others)
        groups = [list(range(parity, experts, 2)) for parity in range(2)]
        returned = lax.all_to_all(
            out.reshape(chips, 2 * capacity, part),
            "expert",
            split_axis=0,
            concat_axis=0,
            axis_index_groups=groups,
        ).reshape(slots, part)
        mixed = jnp.dot(mixers, returned, preferred_element_type=f32).reshape(2, 2, rows, part)
        mixed = mixed[:, 0] + mixed[:, 1]
        state = (state.astype(f32) + mixed[0] + swap(mixed[1], SIBLING)).astype(bf16)
    return state


def solution(mesh):
    placed = (
        P("expert", "tensor"),
        P(None, "tensor"),
        P(None, "tensor", None),
        P(None, "expert", None, "tensor"),
        P(None, "expert", None, "tensor"),
        P(None, "expert", "tensor", None),
        P(None, "expert", None),
    )
    return jax.shard_map(
        body, mesh=mesh, in_specs=placed, out_specs=P("expert", "tensor"), check_vma=False
    )
```

```python
import functools

import jax
import jax.numpy as jnp
from jax import lax
from jax.experimental import pallas as pl
from jax.experimental.pallas import tpu as pltpu
from jax.sharding import PartitionSpec as P

route_scale = 2.5
bf16, f32 = jnp.bfloat16, jnp.float32

Y_STEPS = ((2, 6), (6, 2))
X_STEPS = ((8, 24), (24, 8))
SIBLING = (1, 1)
ORDER = (0, 1, 3, 2)


def short(values):
    return lax.reduce_precision(values, 8, 7)


def thirds(values):
    high = short(values)
    middle = short(values - high)
    return [part.astype(bf16) for part in (high, middle, values - high - middle)]


def swap(block, masks):
    count = lax.axis_size("expert")
    return lax.ppermute(block, "expert", [(i, i ^ masks[i & 1]) for i in range(count)])


def z_swap(block, mask):
    count = lax.axis_size("tensor")
    return lax.ppermute(block, "tensor", [(i, i ^ mask) for i in range(count)])


def after(block, *others):
    return lax.optimization_barrier((block, *others))[0]


def first_kernel(layer, mask, z_ref, own_ref, other_ref, gate_ref, up_ref, out_ref, weights, sems):
    depth, units = weights.shape[1:]
    features = pl.ds(pl.multiple_of((z_ref[0] ^ mask) * depth, depth), depth)
    copies = [
        pltpu.make_async_copy(source.at[layer, 0, features], weights.at[n], sems.at[n])
        for n, source in enumerate((gate_ref, up_ref))
    ]
    for copy in copies:
        copy.start()
    tokens = jnp.concatenate([own_ref[:, :depth], other_ref[:, :depth]], axis=0)
    for n in range(2):
        copies[n].wait()
        product = jnp.dot(tokens, weights[n], preferred_element_type=f32)
        out_ref[:, n * units : (n + 1) * units] = product


def first_products(z, own, other, w_gate, w_up, layer, mask):
    rows, units = 2 * own.shape[0], w_gate.shape[-1]
    depth = w_gate.shape[2] // len(ORDER)
    outside, inside = pl.BlockSpec(memory_space=pl.ANY), pl.BlockSpec(memory_space=pltpu.VMEM)
    return pl.pallas_call(
        functools.partial(first_kernel, layer, mask),
        in_specs=[pl.BlockSpec(memory_space=pltpu.SMEM), inside, inside, outside, outside],
        out_specs=inside,
        out_shape=jax.ShapeDtypeStruct((rows, 2 * units), f32),
        scratch_shapes=[pltpu.VMEM((2, depth, units), bf16), pltpu.SemaphoreType.DMA((2,))],
        compiler_params=pltpu.CompilerParams(vmem_limit_bytes=48 << 20),
        cost_estimate=pl.CostEstimate(
            flops=4 * rows * depth * units,
            bytes_accessed=2 * depth * (rows + 2 * units) + 8 * rows * units,
            transcendentals=0,
        ),
    )(jnp.full((1,), z, jnp.int32), own, other, w_gate, w_up)


def gate_up_kernel(
    layer,
    rows,
    z_ref,
    places_ref,
    tokens_ref,
    taken_ref,
    first_ref,
    gate_ref,
    up_ref,
    act_ref,
    tokens,
    weights,
    sums,
    sems,
):
    steps, depth, units = weights.shape[1:]
    copies = []
    for step, mask in enumerate(ORDER[:steps]):
        features = pl.ds(pl.multiple_of((z_ref[0] ^ mask) * depth, depth), depth)
        parts = [
            (tokens_ref.at[:, pl.ds(step * depth, depth)], tokens.at[step]),
            (gate_ref.at[layer, 0, features], weights.at[0, step]),
            (up_ref.at[layer, 0, features], weights.at[1, step]),
        ]
        copies.append(
            [pltpu.make_async_copy(*part, sems.at[n, step]) for n, part in enumerate(parts)]
        )
    for copy in sum(copies, []):
        copy.start()
    for block in range(sums.shape[0] // rows):
        place = pl.multiple_of(places_ref[block] * rows, rows)
        sums[block * rows : (block + 1) * rows] = first_ref[pl.ds(place, rows)]
    for step in range(steps):
        for copy in copies[step]:
            copy.wait()
        gate = jnp.dot(tokens[step], weights[0, step], preferred_element_type=f32)
        up = jnp.dot(tokens[step], weights[1, step], preferred_element_type=f32)
        if step < steps - 1:
            sums[:, :units] += gate
            sums[:, units:] += up
        else:
            gate += sums[:, :units]
            up += sums[:, units:]
            act = (gate / (1.0 + jnp.exp(-gate)) * up).astype(bf16)
            slots = jnp.dot(taken_ref[...], act, preferred_element_type=f32)
            act_ref[...] = slots.astype(act_ref.dtype)


def gate_up(z, places, tokens, taken, first, w_gate, w_up, layer, block):
    rows, units = tokens.shape[0], w_gate.shape[-1]
    steps = len(ORDER) - 1
    depth = w_gate.shape[2] // len(ORDER)
    outside, inside = pl.BlockSpec(memory_space=pl.ANY), pl.BlockSpec(memory_space=pltpu.VMEM)
    scalars = pl.BlockSpec(memory_space=pltpu.SMEM)
    return pl.pallas_call(
        functools.partial(gate_up_kernel, layer, block),
        in_specs=[scalars, scalars, outside, inside, inside, outside, outside],
        out_specs=inside,
        out_shape=jax.ShapeDtypeStruct((taken.shape[0], units), bf16),
        scratch_shapes=[
            pltpu.VMEM((steps, rows, depth), bf16),
            pltpu.VMEM((2, steps, depth, units), bf16),
            pltpu.VMEM((rows, 2 * units), f32),
            pltpu.SemaphoreType.DMA((3, steps)),
        ],
        compiler_params=pltpu.CompilerParams(vmem_limit_bytes=52 << 20),
        cost_estimate=pl.CostEstimate(
            flops=4 * steps * rows * depth * units,
            bytes_accessed=2 * steps * (rows + 2 * units) * depth + 8 * rows * units,
            transcendentals=rows * units,
        ),
    )(jnp.full((1,), z, jnp.int32), places, tokens, taken, first, w_gate, w_up)


def down_kernel(layer, z_ref, a0, a1, a2, a3, down_ref, w1, w2, w3, out_ref, own, act, sems):
    units, part = own.shape
    column = pl.multiple_of(z_ref[0] * part, part)
    copies = [
        pltpu.make_async_copy(down_ref.at[layer, 0, :, pl.ds(column, part)], own, sems.at[0]),
        pltpu.make_async_copy(a0, act, sems.at[1]),
    ]
    for copy in copies:
        copy.start()
    for copy in copies:
        copy.wait()
    acts = jnp.concatenate([a1[...], a2[...], a3[...], act[...]], axis=1)
    half = part // 2
    for n in range(2):
        columns = slice(n * half, (n + 1) * half)
        weights = jnp.concatenate([w[:, columns] for w in (w1, w2, w3, own)], axis=0)
        out_ref[:, columns] = jnp.dot(acts, weights, preferred_element_type=f32).astype(bf16)


def down_product(z, acts, w_down, layer, others):
    slots, units = acts[0].shape
    part = others[0].shape[-1]
    outside, inside = pl.BlockSpec(memory_space=pl.ANY), pl.BlockSpec(memory_space=pltpu.VMEM)
    return pl.pallas_call(
        functools.partial(down_kernel, layer),
        in_specs=[pl.BlockSpec(memory_space=pltpu.SMEM), outside]
        + [inside] * 3
        + [outside]
        + [inside] * 3,
        out_specs=inside,
        out_shape=jax.ShapeDtypeStruct((slots, part), bf16),
        scratch_shapes=[
            pltpu.VMEM((units, part), bf16),
            pltpu.VMEM((slots, units), bf16),
            pltpu.SemaphoreType.DMA((2,)),
        ],
        compiler_params=pltpu.CompilerParams(vmem_limit_bytes=48 << 20),
        cost_estimate=pl.CostEstimate(
            flops=8 * slots * units * part,
            bytes_accessed=8 * units * (slots + part) + 2 * slots * part,
            transcendentals=0,
        ),
    )(jnp.full((1,), z, jnp.int32), *acts, w_down, *others)


def body(hidden_in, norm_gain, router, w_gate, w_up, w_down, routes):
    rows, part = hidden_in.shape
    layers, width, units = w_gate.shape[0], w_gate.shape[2], w_gate.shape[3]
    experts = router.shape[2]
    capacity = min(rows, 2 * rows * routes.shape[2] // experts)
    slots = experts * capacity
    chips = experts // 2
    quarters = lax.axis_size("tensor")
    me = lax.axis_index("expert")
    core = me & 1
    z = lax.axis_index("tensor")

    away = lax.broadcasted_iota(jnp.int32, (experts,), 0) ^ me
    odd = ((away ^ me) & 1) == 1

    def turns(distance):
        low, high = (distance & 1) ^ (distance >> 1), distance >> 1
        return jnp.where(odd, high, low) + 2 * jnp.where(odd, low, high)

    places = (away & 1) * chips + turns((away >> 1) & 3) + 4 * turns(away >> 3)
    in_place = places[:, None] == lax.broadcasted_iota(jnp.int32, (1, experts), 1)

    expert_iota = lax.broadcasted_iota(jnp.int32, (1, 1, 1, experts), 3)
    picks = jnp.any(routes[..., None] == expert_iota, axis=2)
    earlier = lax.broadcasted_iota(jnp.int32, (rows, rows), 0) >= lax.broadcasted_iota(
        jnp.int32, (rows, rows), 1
    )
    ranks = jnp.einsum("st,lte->lse", earlier.astype(bf16), picks.astype(bf16), preferred_element_type=f32)
    marks = jnp.where(picks, ranks, 0.0)
    marks_sent = jnp.concatenate([marks[layer] for layer in range(layers)], axis=1)
    marks_sent = jnp.pad(marks_sent, ((0, 0), (0, 128 - layers * experts))).astype(bf16)

    def spread(block):
        return [block] + [z_swap(block, mask) for mask in ORDER[1:]]

    def columns(layer, mask, *bound):
        column = (after(z, *bound) ^ mask) * part
        block = lax.dynamic_slice(w_down, (layer, 0, 0, column), (1, 1, units, part))
        return block.reshape(units, part)

    def slots_of(marks_here, layer):
        mine = lax.broadcasted_iota(jnp.int32, (1, 1, 128), 2) == me + layer * experts
        mark = jnp.sum(jnp.where(mine, marks_here, 0.0), axis=2).astype(bf16)
        mark = jnp.dot(in_place.astype(bf16), mark, preferred_element_type=f32).astype(jnp.int32)
        source = lax.broadcasted_iota(jnp.int32, (experts, 1), 0)
        slot = jnp.where(mark > 0, source * capacity + mark - 1, -1).reshape(1, -1)
        return (lax.broadcasted_iota(jnp.int32, (slots, 1), 0) == slot).astype(bf16)

    state = hidden_in
    gains = jnp.stack(thirds(norm_gain), axis=0).reshape(3 * layers, part)
    opening = [state, gains, jnp.zeros((8 - 3 * layers, part), bf16)]
    opening = spread(jnp.concatenate(opening, axis=0))
    gains = [
        block[rows : rows + 3 * layers].astype(f32).reshape(3, layers, part).sum(axis=0)
        for block in opening
    ]
    for layer in range(layers):
        blocks = spread(state) if layer else [block[:rows] for block in opening]
        blocks = [block.astype(f32) for block in blocks]
        scale = sum(jnp.sum(block * block, axis=1) for block in blocks)
        scale = lax.rsqrt(scale / width + 1e-06)
        normed = [
            (block * scale[:, None] * gain[layer][None, :]).astype(bf16)
            for block, gain in zip(blocks, gains)
        ]

        sent = jnp.concatenate(normed[:3], axis=1)
        arrived = lax.all_gather(sent, "expert", axis=0, tiled=True)

        own = state.astype(f32) * scale[:, None] * norm_gain[layer][None, :]
        own = own.astype(bf16).astype(f32)
        scores = jnp.dot(own, router[layer], precision=lax.Precision.HIGHEST)
        scores = after(scores, sent)
        probs = jax.nn.sigmoid(sum(spread(scores)))
        picked = jnp.where(picks[layer], probs, 0.0)
        weights = route_scale * picked / jnp.sum(picked, axis=1, keepdims=True)

        def mixer(parity):
            def of_parity(table):
                table = table.reshape(rows, chips, 2)
                return jnp.where(parity == 1, table[:, :, 1], table[:, :, 0])[:, :, None, None]

            shape = (1, 1, 2, capacity)
            slot = lax.broadcasted_iota(jnp.int32, shape, 3).astype(f32) + 1.0
            here = lax.broadcasted_iota(jnp.int32, shape, 2) == core
            table = jnp.where(here & (of_parity(marks[layer]) == slot), of_parity(weights), 0.0)
            return jnp.concatenate(thirds(table.reshape(rows, slots))[:2], axis=0)

        mixers = jnp.concatenate([mixer(core), swap(mixer(1 - core), SIBLING)], axis=0)

        held = after(normed[3], sent)
        held = (jnp.concatenate([held, marks_sent], axis=1) if layer == 0 else held)[None]
        blocks = [columns(layer, mask, held) for mask in ORDER[1:]]
        near = [z_swap(block, mask) for block, mask in zip(blocks[:2], ORDER[1:3])]
        for step, masks in enumerate(Y_STEPS + X_STEPS):
            if step == 3:
                held, far, near = lax.optimization_barrier((held, blocks[2], near))
                far = z_swap(far, ORDER[3])
            held = jnp.concatenate([held, swap(held, masks)])
        held, far = lax.optimization_barrier((held, far))
        others = near + [far]
        swapped = swap(held, SIBLING)
        if layer == 0:
            marks_all = jnp.concatenate([held[:, :, part:], swapped[:, :, part:]]).astype(f32)
            taken = [slots_of(marks_all, each) for each in range(layers)]
        flat = [block.reshape(chips * rows, -1) for block in (held, swapped)]
        first = first_products(z, *flat, w_gate, w_up, layer, ORDER[3])
        arrived, mixers, first, taken, others = lax.optimization_barrier(
            (arrived, mixers, first, taken, others)
        )
        act = gate_up(z, places, arrived, taken[layer], first, w_gate, w_up, layer, rows)
        acts = spread(act)
        acts[0] = jnp.where(z < quarters, acts[0], 0.0)
        out = down_product(z, acts, w_down, layer, others)
        groups = [list(range(parity, experts, 2)) for parity in range(2)]
        returned = lax.all_to_all(
            out.reshape(chips, 2 * capacity, part),
            "expert",
            split_axis=0,
            concat_axis=0,
            axis_index_groups=groups,
        ).reshape(slots, part)
        mixed = jnp.dot(mixers, returned, preferred_element_type=f32).reshape(2, 2, rows, part)
        mixed = mixed[:, 0] + mixed[:, 1]
        state = (state.astype(f32) + mixed[0] + swap(mixed[1], SIBLING)).astype(bf16)
    return state


def solution(mesh):
    placed = (
        P("expert", "tensor"),
        P(None, "tensor"),
        P(None, "tensor", None),
        P(None, "expert", None, "tensor"),
        P(None, "expert", None, "tensor"),
        P(None, "expert", "tensor", None),
        P(None, "expert", None),
    )
    return jax.shard_map(
        body, mesh=mesh, in_specs=placed, out_specs=P("expert", "tensor"), check_vma=False
    )
```

```python
import functools

import jax
import jax.numpy as jnp
from jax import lax
from jax.experimental import pallas as pl
from jax.experimental.pallas import tpu as pltpu
from jax.sharding import PartitionSpec as P

route_scale = 2.5
bf16, f32 = jnp.bfloat16, jnp.float32

Y_STEPS = ((2, 6), (6, 2))
X_STEPS = ((8, 24), (24, 8))
SIBLING = (1, 1)
ORDER = (0, 1, 3, 2)


def short(values):
    return lax.reduce_precision(values, 8, 7)


def thirds(values):
    high = short(values)
    middle = short(values - high)
    return [part.astype(bf16) for part in (high, middle, values - high - middle)]


def swap(block, masks):
    count = lax.axis_size("expert")
    return lax.ppermute(block, "expert", [(i, i ^ masks[i & 1]) for i in range(count)])


def z_swap(block, mask):
    count = lax.axis_size("tensor")
    return lax.ppermute(block, "tensor", [(i, i ^ mask) for i in range(count)])


def after(block, *others):
    return lax.optimization_barrier((block, *others))[0]


def gate_up_kernel(
    layer, z_ref, tokens_ref, taken_ref, gate_ref, up_ref, act_ref, tokens, weights, sums, sems
):
    steps, depth = weights.shape[1:3]
    copies = []
    for step, mask in enumerate(ORDER):
        features = pl.ds(pl.multiple_of((z_ref[0] ^ mask) * depth, depth), depth)
        parts = [
            (tokens_ref.at[:, pl.ds(step * depth, depth)], tokens.at[step]),
            (gate_ref.at[layer, 0, features], weights.at[0, step]),
            (up_ref.at[layer, 0, features], weights.at[1, step]),
        ]
        copies.append(
            [pltpu.make_async_copy(*part, sems.at[n, step]) for n, part in enumerate(parts)]
        )
    for copy in sum(copies, []):
        copy.start()
    for step in range(steps):
        for copy in copies[step]:
            copy.wait()
        gate = jnp.dot(tokens[step], weights[0, step], preferred_element_type=f32)
        up = jnp.dot(tokens[step], weights[1, step], preferred_element_type=f32)
        if step == 0:
            sums[0], sums[1] = gate, up
        elif step < steps - 1:
            sums[0] += gate
            sums[1] += up
        else:
            gate += sums[0]
            up += sums[1]
            act = (gate / (1.0 + jnp.exp(-gate)) * up).astype(bf16)
            slots = jnp.dot(taken_ref[...], act, preferred_element_type=f32)
            act_ref[...] = slots.astype(act_ref.dtype)


def gate_up(z, tokens, taken, w_gate, w_up, layer):
    rows, units = tokens.shape[0], w_gate.shape[-1]
    steps = len(ORDER)
    depth = w_gate.shape[2] // steps
    outside, inside = pl.BlockSpec(memory_space=pl.ANY), pl.BlockSpec(memory_space=pltpu.VMEM)
    return pl.pallas_call(
        functools.partial(gate_up_kernel, layer),
        in_specs=[pl.BlockSpec(memory_space=pltpu.SMEM), outside, inside, outside, outside],
        out_specs=inside,
        out_shape=jax.ShapeDtypeStruct((taken.shape[0], units), bf16),
        scratch_shapes=[
            pltpu.VMEM((steps, rows, depth), bf16),
            pltpu.VMEM((2, steps, depth, units), bf16),
            pltpu.VMEM((2, rows, units), f32),
            pltpu.SemaphoreType.DMA((3, steps)),
        ],
        compiler_params=pltpu.CompilerParams(vmem_limit_bytes=56 << 20),
        cost_estimate=pl.CostEstimate(
            flops=16 * rows * depth * units,
            bytes_accessed=8 * (rows + 2 * units) * depth + 2 * rows * units,
            transcendentals=rows * units,
        ),
    )(jnp.full((1,), z, jnp.int32), tokens, taken, w_gate, w_up)


def down_kernel(layer, z_ref, a0, a1, a2, a3, down_ref, w1, w2, w3, out_ref, own, act, sems):
    units, part = own.shape
    column = pl.multiple_of(z_ref[0] * part, part)
    copies = [
        pltpu.make_async_copy(down_ref.at[layer, 0, :, pl.ds(column, part)], own, sems.at[0]),
        pltpu.make_async_copy(a0, act, sems.at[1]),
    ]
    for copy in copies:
        copy.start()
    for copy in copies:
        copy.wait()
    acts = jnp.concatenate([a1[...], a2[...], a3[...], act[...]], axis=1)
    half = part // 2
    for n in range(2):
        columns = slice(n * half, (n + 1) * half)
        weights = jnp.concatenate([w[:, columns] for w in (w1, w2, w3, own)], axis=0)
        out_ref[:, columns] = jnp.dot(acts, weights, preferred_element_type=f32).astype(bf16)


def down_product(z, acts, w_down, layer, others):
    slots, units = acts[0].shape
    part = others[0].shape[-1]
    outside, inside = pl.BlockSpec(memory_space=pl.ANY), pl.BlockSpec(memory_space=pltpu.VMEM)
    return pl.pallas_call(
        functools.partial(down_kernel, layer),
        in_specs=[pl.BlockSpec(memory_space=pltpu.SMEM), outside]
        + [inside] * 3
        + [outside]
        + [inside] * 3,
        out_specs=inside,
        out_shape=jax.ShapeDtypeStruct((slots, part), bf16),
        scratch_shapes=[
            pltpu.VMEM((units, part), bf16),
            pltpu.VMEM((slots, units), bf16),
            pltpu.SemaphoreType.DMA((2,)),
        ],
        compiler_params=pltpu.CompilerParams(vmem_limit_bytes=48 << 20),
        cost_estimate=pl.CostEstimate(
            flops=8 * slots * units * part,
            bytes_accessed=8 * units * (slots + part) + 2 * slots * part,
            transcendentals=0,
        ),
    )(jnp.full((1,), z, jnp.int32), *acts, w_down, *others)


def body(hidden_in, norm_gain, router, w_gate, w_up, w_down, routes):
    rows, part = hidden_in.shape
    layers, width, units = w_gate.shape[0], w_gate.shape[2], w_gate.shape[3]
    experts = router.shape[2]
    capacity = min(rows, 2 * rows * routes.shape[2] // experts)
    slots = experts * capacity
    chips = experts // 2
    quarters = lax.axis_size("tensor")
    me = lax.axis_index("expert")
    core = me & 1
    z = lax.axis_index("tensor")

    away = lax.broadcasted_iota(jnp.int32, (experts,), 0) ^ me
    odd = ((away ^ me) & 1) == 1

    def turns(distance):
        low, high = (distance & 1) ^ (distance >> 1), distance >> 1
        return jnp.where(odd, high, low) + 2 * jnp.where(odd, low, high)

    places = (away & 1) * chips + turns((away >> 1) & 3) + 4 * turns(away >> 3)
    in_place = places[:, None] == lax.broadcasted_iota(jnp.int32, (1, experts), 1)

    expert_iota = lax.broadcasted_iota(jnp.int32, (1, 1, 1, experts), 3)
    picks = jnp.any(routes[..., None] == expert_iota, axis=2)
    earlier = lax.broadcasted_iota(jnp.int32, (rows, rows), 0) >= lax.broadcasted_iota(
        jnp.int32, (rows, rows), 1
    )
    ranks = jnp.einsum("st,lte->lse", earlier.astype(bf16), picks.astype(bf16), preferred_element_type=f32)
    marks = jnp.where(picks, ranks, 0.0)
    marks_sent = jnp.concatenate([marks[layer] for layer in range(layers)], axis=1)
    marks_sent = jnp.pad(marks_sent, ((0, 0), (0, 128 - layers * experts))).astype(bf16)

    def spread(block):
        return [block] + [z_swap(block, mask) for mask in ORDER[1:]]

    def columns(layer, mask, first, count, *bound):
        column = (after(z, *bound) ^ mask) * part
        block = lax.dynamic_slice(w_down, (layer, 0, first, column), (1, 1, count, part))
        return z_swap(block.reshape(count, part), mask)

    def slots_of(marks_here, layer):
        mine = lax.broadcasted_iota(jnp.int32, (1, 1, 128), 2) == me + layer * experts
        mark = jnp.sum(jnp.where(mine, marks_here, 0.0), axis=2).astype(bf16)
        mark = jnp.dot(in_place.astype(bf16), mark, preferred_element_type=f32).astype(jnp.int32)
        source = lax.broadcasted_iota(jnp.int32, (experts, 1), 0)
        slot = jnp.where(mark > 0, source * capacity + mark - 1, -1).reshape(1, -1)
        return (lax.broadcasted_iota(jnp.int32, (slots, 1), 0) == slot).astype(bf16)

    state = hidden_in
    gains = spread(norm_gain)
    for layer in range(layers):
        blocks = [block.astype(f32) for block in spread(state)]
        scale = sum(jnp.sum(block * block, axis=1) for block in blocks)
        scale = lax.rsqrt(scale / width + 1e-06)
        normed = [
            (block * scale[:, None] * gain[layer][None, :]).astype(bf16)
            for block, gain in zip(blocks, gains)
        ]

        sent = jnp.concatenate(normed, axis=1)
        arrived = lax.all_gather(sent, "expert", axis=0, tiled=True)

        own = state.astype(f32) * scale[:, None] * norm_gain[layer][None, :]
        own = own.astype(bf16).astype(f32)
        scores = jnp.dot(own, router[layer], precision=lax.Precision.HIGHEST)
        scores = after(scores, sent)
        others = [columns(layer, mask, 0, units, scores) for mask in ORDER[1:]]
        probs = jax.nn.sigmoid(sum(spread(scores)))
        picked = jnp.where(picks[layer], probs, 0.0)
        weights = route_scale * picked / jnp.sum(picked, axis=1, keepdims=True)

        def mixer(parity):
            def of_parity(table):
                table = table.reshape(rows, chips, 2)
                return jnp.where(parity == 1, table[:, :, 1], table[:, :, 0])[:, :, None, None]

            shape = (1, 1, 2, capacity)
            slot = lax.broadcasted_iota(jnp.int32, shape, 3).astype(f32) + 1.0
            here = lax.broadcasted_iota(jnp.int32, shape, 2) == core
            table = jnp.where(here & (of_parity(marks[layer]) == slot), of_parity(weights), 0.0)
            return jnp.concatenate(thirds(table.reshape(rows, slots))[:2], axis=0)

        mixers = jnp.concatenate([mixer(core), swap(mixer(1 - core), SIBLING)], axis=0)

        if layer == 0:
            held = after(marks_sent, scores)[None]
            for masks in Y_STEPS + X_STEPS:
                held = jnp.concatenate([held, swap(held, masks)])
            held = jnp.concatenate([held, swap(held, SIBLING)]).astype(f32)
            taken = [slots_of(held, each) for each in range(layers)]
            arrived, mixers, taken, others = lax.optimization_barrier(
                (arrived, mixers, taken, others)
            )
        else:
            arrived, mixers, others = lax.optimization_barrier((arrived, mixers, others))
        acts = spread(gate_up(z, arrived, taken[layer], w_gate, w_up, layer))
        acts[0] = jnp.where(z < quarters, acts[0], 0.0)
        out = down_product(z, acts, w_down, layer, others)
        groups = [list(range(parity, experts, 2)) for parity in range(2)]
        returned = lax.all_to_all(
            out.reshape(chips, 2 * capacity, part),
            "expert",
            split_axis=0,
            concat_axis=0,
            axis_index_groups=groups,
        ).reshape(slots, part)
        mixed = jnp.dot(mixers, returned, preferred_element_type=f32).reshape(2, 2, rows, part)
        mixed = mixed[:, 0] + mixed[:, 1]
        state = (state.astype(f32) + mixed[0] + swap(mixed[1], SIBLING)).astype(bf16)
    return state


def solution(mesh):
    placed = (
        P("expert", "tensor"),
        P(None, "tensor"),
        P(None, "tensor", None),
        P(None, "expert", None, "tensor"),
        P(None, "expert", None, "tensor"),
        P(None, "expert", "tensor", None),
        P(None, "expert", None),
    )
    return jax.shard_map(
        body, mesh=mesh, in_specs=placed, out_specs=P("expert", "tensor"), check_vma=False
    )
```

```python
import functools

import jax
import jax.numpy as jnp
from jax import lax
from jax.experimental import pallas as pl
from jax.experimental.pallas import tpu as pltpu
from jax.sharding import PartitionSpec as P

route_scale = 2.5
bf16, f32 = jnp.bfloat16, jnp.float32

Y_STEPS = ((2, 6), (6, 2))
X_STEPS = ((8, 24), (24, 8))
SIBLING = (1, 1)
ORDER = (0, 1, 3, 2)


def short(values):
    return lax.reduce_precision(values, 8, 7)


def thirds(values):
    high = short(values)
    middle = short(values - high)
    return [part.astype(bf16) for part in (high, middle, values - high - middle)]


def swap(block, masks):
    count = lax.axis_size("expert")
    return lax.ppermute(block, "expert", [(i, i ^ masks[i & 1]) for i in range(count)])


def z_swap(block, mask):
    count = lax.axis_size("tensor")
    return lax.ppermute(block, "tensor", [(i, i ^ mask) for i in range(count)])


def after(block, *others):
    return lax.optimization_barrier((block, *others))[0]


def opening_kernel(state_ref, gain_ref, out_ref):
    gain = gain_ref[...]
    high = gain.astype(bf16).astype(f32)
    middle = (gain - high).astype(bf16).astype(f32)
    parts = [state_ref[...].astype(f32), high, middle, gain - high - middle]
    rest = out_ref.shape[0] - sum(part.shape[0] for part in parts)
    parts.append(jnp.zeros((rest, out_ref.shape[1]), f32))
    out_ref[...] = jnp.concatenate(parts, axis=0).astype(bf16)


def join(state, gain):
    inside = pl.BlockSpec(memory_space=pltpu.VMEM)
    return pl.pallas_call(
        opening_kernel,
        in_specs=[inside, inside],
        out_specs=inside,
        out_shape=jax.ShapeDtypeStruct((state.shape[0] + 8, state.shape[1]), bf16),
    )(state, gain)


def norm_kernel(layer, layers, b0, b1, b2, b3, g0, g1, g2, g3, out_ref, scale_ref):
    rows, width = out_ref.shape
    part = width // len(ORDER)
    blocks = [block[...].astype(f32)[:rows] for block in (b0, b1, b2, b3)]
    scale = sum(jnp.sum(block * block, axis=1, keepdims=True) for block in blocks)
    scale = lax.rsqrt(scale / width + 1e-06)
    scale_ref[...] = jnp.broadcast_to(scale, scale_ref.shape)
    for n, (block, gains) in enumerate(zip(blocks, (g0, g1, g2, g3))):
        terms = gains[...].astype(f32)[rows:]
        gain = sum(terms[k * layers + layer : k * layers + layer + 1] for k in range(3))
        out_ref[:, n * part : (n + 1) * part] = (block * scale * gain).astype(bf16)


def normalize(blocks, openings, rows, layer, layers):
    inside = pl.BlockSpec(memory_space=pltpu.VMEM)
    width = len(blocks) * blocks[0].shape[1]
    normed, scale = pl.pallas_call(
        functools.partial(norm_kernel, layer, layers),
        in_specs=[inside] * 8,
        out_specs=(inside, inside),
        out_shape=(
            jax.ShapeDtypeStruct((rows, width), bf16),
            jax.ShapeDtypeStruct((rows, 128), f32),
        ),
    )(*blocks, *openings)
    return normed, scale[:, 0]


def gate_up_kernel(
    layer, z_ref, tokens_ref, taken_ref, gate_ref, up_ref, act_ref, tokens, weights, sums, sems
):
    steps, depth = weights.shape[1:3]
    copies = []
    for step, mask in enumerate(ORDER):
        features = pl.ds(pl.multiple_of((z_ref[0] ^ mask) * depth, depth), depth)
        parts = [
            (tokens_ref.at[:, pl.ds(step * depth, depth)], tokens.at[step]),
            (gate_ref.at[layer, 0, features], weights.at[0, step]),
            (up_ref.at[layer, 0, features], weights.at[1, step]),
        ]
        copies.append(
            [pltpu.make_async_copy(*part, sems.at[n, step]) for n, part in enumerate(parts)]
        )
    for copy in sum(copies, []):
        copy.start()
    for step in range(steps):
        for copy in copies[step]:
            copy.wait()
        gate = jnp.dot(tokens[step], weights[0, step], preferred_element_type=f32)
        up = jnp.dot(tokens[step], weights[1, step], preferred_element_type=f32)
        if step == 0:
            sums[0], sums[1] = gate, up
        elif step < steps - 1:
            sums[0] += gate
            sums[1] += up
        else:
            gate += sums[0]
            up += sums[1]
            act = (gate / (1.0 + jnp.exp(-gate)) * up).astype(bf16)
            slots = jnp.dot(taken_ref[...], act, preferred_element_type=f32)
            act_ref[...] = slots.astype(act_ref.dtype)


def gate_up(z, tokens, taken, w_gate, w_up, layer):
    rows, units = tokens.shape[0], w_gate.shape[-1]
    steps = len(ORDER)
    depth = w_gate.shape[2] // steps
    outside, inside = pl.BlockSpec(memory_space=pl.ANY), pl.BlockSpec(memory_space=pltpu.VMEM)
    return pl.pallas_call(
        functools.partial(gate_up_kernel, layer),
        in_specs=[pl.BlockSpec(memory_space=pltpu.SMEM), outside, inside, outside, outside],
        out_specs=inside,
        out_shape=jax.ShapeDtypeStruct((taken.shape[0], units), bf16),
        scratch_shapes=[
            pltpu.VMEM((steps, rows, depth), bf16),
            pltpu.VMEM((2, steps, depth, units), bf16),
            pltpu.VMEM((2, rows, units), f32),
            pltpu.SemaphoreType.DMA((3, steps)),
        ],
        compiler_params=pltpu.CompilerParams(vmem_limit_bytes=56 << 20),
        cost_estimate=pl.CostEstimate(
            flops=16 * rows * depth * units,
            bytes_accessed=8 * (rows + 2 * units) * depth + 2 * rows * units,
            transcendentals=rows * units,
        ),
    )(jnp.full((1,), z, jnp.int32), tokens, taken, w_gate, w_up)


def down_kernel(layer, z_ref, a0, a1, a2, a3, down_ref, w1, w2, w3, out_ref, own, act, sems):
    units, part = own.shape
    column = pl.multiple_of(z_ref[0] * part, part)
    copies = [
        pltpu.make_async_copy(down_ref.at[layer, 0, :, pl.ds(column, part)], own, sems.at[0]),
        pltpu.make_async_copy(a0, act, sems.at[1]),
    ]
    for copy in copies:
        copy.start()
    for copy in copies:
        copy.wait()
    acts = jnp.concatenate([a1[...], a2[...], a3[...], act[...]], axis=1)
    half = part // 2
    for n in range(2):
        columns = slice(n * half, (n + 1) * half)
        weights = jnp.concatenate([w[:, columns] for w in (w1, w2, w3, own)], axis=0)
        out_ref[:, columns] = jnp.dot(acts, weights, preferred_element_type=f32).astype(bf16)


def down_product(z, acts, w_down, layer, others):
    slots, units = acts[0].shape
    part = others[0].shape[-1]
    outside, inside = pl.BlockSpec(memory_space=pl.ANY), pl.BlockSpec(memory_space=pltpu.VMEM)
    return pl.pallas_call(
        functools.partial(down_kernel, layer),
        in_specs=[pl.BlockSpec(memory_space=pltpu.SMEM), outside]
        + [inside] * 3
        + [outside]
        + [inside] * 3,
        out_specs=inside,
        out_shape=jax.ShapeDtypeStruct((slots, part), bf16),
        scratch_shapes=[
            pltpu.VMEM((units, part), bf16),
            pltpu.VMEM((slots, units), bf16),
            pltpu.SemaphoreType.DMA((2,)),
        ],
        compiler_params=pltpu.CompilerParams(vmem_limit_bytes=48 << 20),
        cost_estimate=pl.CostEstimate(
            flops=8 * slots * units * part,
            bytes_accessed=8 * units * (slots + part) + 2 * slots * part,
            transcendentals=0,
        ),
    )(jnp.full((1,), z, jnp.int32), *acts, w_down, *others)


def body(hidden_in, norm_gain, router, w_gate, w_up, w_down, routes):
    rows, part = hidden_in.shape
    layers, width, units = w_gate.shape[0], w_gate.shape[2], w_gate.shape[3]
    experts = router.shape[2]
    capacity = min(rows, 2 * rows * routes.shape[2] // experts)
    slots = experts * capacity
    chips = experts // 2
    quarters = lax.axis_size("tensor")
    me = lax.axis_index("expert")
    core = me & 1
    z = lax.axis_index("tensor")

    away = lax.broadcasted_iota(jnp.int32, (experts,), 0) ^ me
    odd = ((away ^ me) & 1) == 1

    def turns(distance):
        low, high = (distance & 1) ^ (distance >> 1), distance >> 1
        return jnp.where(odd, high, low) + 2 * jnp.where(odd, low, high)

    places = (away & 1) * chips + turns((away >> 1) & 3) + 4 * turns(away >> 3)
    in_place = places[:, None] == lax.broadcasted_iota(jnp.int32, (1, experts), 1)

    expert_iota = lax.broadcasted_iota(jnp.int32, (1, 1, 1, experts), 3)
    picks = jnp.any(routes[..., None] == expert_iota, axis=2)
    earlier = lax.broadcasted_iota(jnp.int32, (rows, rows), 0) >= lax.broadcasted_iota(
        jnp.int32, (rows, rows), 1
    )
    ranks = jnp.einsum("st,lte->lse", earlier.astype(bf16), picks.astype(bf16), preferred_element_type=f32)
    marks = jnp.where(picks, ranks, 0.0)
    marks_sent = jnp.concatenate([marks[layer] for layer in range(layers)], axis=1)
    marks_sent = jnp.pad(marks_sent, ((0, 0), (0, 128 - layers * experts))).astype(bf16)

    def spread(block):
        return [block] + [z_swap(block, mask) for mask in ORDER[1:]]

    def columns(layer, mask, first, count, *bound):
        column = (after(z, *bound) ^ mask) * part
        block = lax.dynamic_slice(w_down, (layer, 0, first, column), (1, 1, count, part))
        return z_swap(block.reshape(count, part), mask)

    def slots_of(marks_here, layer):
        mine = lax.broadcasted_iota(jnp.int32, (1, 1, 128), 2) == me + layer * experts
        mark = jnp.sum(jnp.where(mine, marks_here, 0.0), axis=2).astype(bf16)
        mark = jnp.dot(in_place.astype(bf16), mark, preferred_element_type=f32).astype(jnp.int32)
        source = lax.broadcasted_iota(jnp.int32, (experts, 1), 0)
        slot = jnp.where(mark > 0, source * capacity + mark - 1, -1).reshape(1, -1)
        return (lax.broadcasted_iota(jnp.int32, (slots, 1), 0) == slot).astype(bf16)

    state = hidden_in
    openings = spread(join(state, norm_gain))
    for layer in range(layers):
        blocks = spread(state) if layer else openings
        sent, scale = normalize(blocks, openings, rows, layer, layers)
        arrived = lax.all_gather(sent, "expert", axis=0, tiled=True)

        own = state.astype(f32) * scale[:, None] * norm_gain[layer][None, :]
        own = own.astype(bf16).astype(f32)
        scores = jnp.dot(own, router[layer], precision=lax.Precision.HIGHEST)
        scores = after(scores, sent)
        others = [columns(layer, mask, 0, units, scores) for mask in ORDER[1:]]
        probs = jax.nn.sigmoid(sum(spread(scores)))
        picked = jnp.where(picks[layer], probs, 0.0)
        weights = route_scale * picked / jnp.sum(picked, axis=1, keepdims=True)

        def mixer(parity):
            def of_parity(table):
                table = table.reshape(rows, chips, 2)
                return jnp.where(parity == 1, table[:, :, 1], table[:, :, 0])[:, :, None, None]

            shape = (1, 1, 2, capacity)
            slot = lax.broadcasted_iota(jnp.int32, shape, 3).astype(f32) + 1.0
            here = lax.broadcasted_iota(jnp.int32, shape, 2) == core
            table = jnp.where(here & (of_parity(marks[layer]) == slot), of_parity(weights), 0.0)
            return jnp.concatenate(thirds(table.reshape(rows, slots))[:2], axis=0)

        mixers = jnp.concatenate([mixer(core), swap(mixer(1 - core), SIBLING)], axis=0)

        if layer == 0:
            held = after(marks_sent, scores)[None]
            for masks in Y_STEPS + X_STEPS:
                held = jnp.concatenate([held, swap(held, masks)])
            held = jnp.concatenate([held, swap(held, SIBLING)]).astype(f32)
            taken = [slots_of(held, each) for each in range(layers)]
            arrived, mixers, taken, others = lax.optimization_barrier(
                (arrived, mixers, taken, others)
            )
        else:
            arrived, mixers, others = lax.optimization_barrier((arrived, mixers, others))
        acts = spread(gate_up(z, arrived, taken[layer], w_gate, w_up, layer))
        acts[0] = jnp.where(z < quarters, acts[0], 0.0)
        out = down_product(z, acts, w_down, layer, others)
        groups = [list(range(parity, experts, 2)) for parity in range(2)]
        returned = lax.all_to_all(
            out.reshape(chips, 2 * capacity, part),
            "expert",
            split_axis=0,
            concat_axis=0,
            axis_index_groups=groups,
        ).reshape(slots, part)
        mixed = jnp.dot(mixers, returned, preferred_element_type=f32).reshape(2, 2, rows, part)
        mixed = mixed[:, 0] + mixed[:, 1]
        state = (state.astype(f32) + mixed[0] + swap(mixed[1], SIBLING)).astype(bf16)
    return state


def solution(mesh):
    placed = (
        P("expert", "tensor"),
        P(None, "tensor"),
        P(None, "tensor", None),
        P(None, "expert", None, "tensor"),
        P(None, "expert", None, "tensor"),
        P(None, "expert", "tensor", None),
        P(None, "expert", None),
    )
    return jax.shard_map(
        body, mesh=mesh, in_specs=placed, out_specs=P("expert", "tensor"), check_vma=False
    )
```
